128 devices in a mesh: batch: 8 (over x, core), feat: 16 (over y, z).
Axes of the slice: x: 4, y: 4, z: 4, core: 2. Of those that a mesh axis runs over, the one named last changes fastest.
Arguments:
- view_a: bfloat16 [4096, 8192], P('batch', 'feat'), may hold values from -800 to 800
- view_b: bfloat16 [4096, 8192], P('batch', 'feat'), may hold values from -800 to 800
Outputs:
- grad_a: bfloat16 [4096, 8192], P('batch', 'feat')
- grad_b: bfloat16 [4096, 8192], P('batch', 'feat')
The draws below stay inside these ranges and needn't reach their ends.
All inputs are finite; a program needn't handle non-finite values.
Results may differ from the reference program's by a relative error of at most 0.0069.
Values may be sent and summed in bfloat16 or wider, within the bound.
A program may use at most 128 MiB of HBM per device.

```python
import math
import jax
import jax.numpy as jnp
from jax import lax

D = 8192
PAIRS = 4096


def shared_parts(key, spread_load):
    keys = jax.random.split(key, 7)
    groups = 128
    factor_one = jnp.clip(jax.random.normal(keys[0], (PAIRS, groups), jnp.float32), -4.0, 4.0)
    factor_two = jnp.clip(jax.random.normal(keys[5], (PAIRS, groups), jnp.float32), -4.0, 4.0)
    spread_one = jnp.tile(factor_one, (1, D // groups))
    spread_two = jnp.repeat(factor_two, D // groups, axis=1)
    load_one = jax.random.uniform(keys[4], (1, D), jnp.float32, -spread_load, spread_load)
    load_two = jax.random.uniform(keys[6], (1, D), jnp.float32, -spread_load, spread_load)
    common = load_one * spread_one + load_two * spread_two
    gauss = jnp.clip(jax.random.normal(keys[1], (PAIRS, D), jnp.float32), -4.0, 4.0)
    noise = gauss
    position = jnp.arange(PAIRS, dtype=jnp.float32)[:, None] / PAIRS
    rough = jnp.exp(jax.random.uniform(keys[3], (PAIRS, 1), jnp.float32, math.log(0.7), math.log(1.4)))
    row_scale = jnp.exp(position * math.log(3.0)) * rough
    return (common, noise, row_scale)


def feature_terms(key, top_scale):
    keys = jax.random.split(key, 2)
    offset = jax.random.uniform(keys[0], (1, D), jnp.float32, -2.0, 2.0)
    scales = jnp.exp(jax.random.uniform(keys[1], (1, D), jnp.float32, 0.0, math.log(top_scale)))
    return (offset, scales)


def draw_view_a(key, part):
    common, noise, row_scale = shared_parts(key, 1.5)
    offset, scales = feature_terms(jax.random.fold_in(key, 11), 10.0)
    values = offset + scales * row_scale * (common + noise)
    return values.astype(jnp.bfloat16)


def draw_view_b(key, part):
    common, noise, row_scale = shared_parts(key, 1.5)
    offset, scales = feature_terms(jax.random.fold_in(key, 23), 10.0)
    fresh = jnp.clip(jax.random.normal(jax.random.fold_in(key, 37), (PAIRS, D), jnp.float32), -4.0, 4.0)
    values = offset + scales * row_scale * (common + 0.8 * noise + 0.6 * fresh)
    return values.astype(jnp.bfloat16)


def setup_inputs(seed: int = 0) -> dict:
    seeds = jax.random.split(jax.random.key(seed), 3)
    return {
        "view_a": draw_view_a(jax.random.fold_in(seeds[2], 71), 0),
        "view_b": draw_view_b(jax.random.fold_in(seeds[2], 71), 0),
    }


def normalize(view):
    values = view.astype(jnp.float32)
    average = lax.optimization_barrier(jnp.mean(values, axis=0))
    square = lax.optimization_barrier(jnp.mean(values * values, axis=0))
    scales = lax.rsqrt(square - average * average + 1e-05)
    unit = (values - average) * scales
    return (unit, scales)

def backward(back, unit, scales):
    first = lax.optimization_barrier(jnp.mean(back, axis=0))
    second = lax.optimization_barrier(jnp.mean(back * unit, axis=0))
    return (scales * (back - first - unit * second)).astype(jnp.bfloat16)

def reference(view_a, view_b):
    unit_a, scales_a = normalize(view_a)
    unit_b, scales_b = normalize(view_b)
    normed_a = unit_a.astype(jnp.bfloat16)
    normed_b = unit_b.astype(jnp.bfloat16)
    corr = jnp.dot(normed_a.T, normed_b, preferred_element_type=jnp.float32) / PAIRS
    index = jnp.arange(D, dtype=jnp.int32)
    same = index[:, None] == index[None, :]
    penalty = jnp.where(same, 2.0 * (corr - 1.0), 2.0 * 0.0051 * corr).astype(jnp.bfloat16)
    back_a = jnp.dot(normed_b, penalty.T, preferred_element_type=jnp.float32)
    back_b = jnp.dot(normed_a, penalty, preferred_element_type=jnp.float32)
    return (backward(back_a, unit_a, scales_a), backward(back_b, unit_b, scales_b))
```

```python
import jax
import jax.numpy as jnp
from jax import lax
from jax.sharding import PartitionSpec as P

LAMBDA = 0.0051


def normalize(whole, total):
    values = whole.astype(jnp.float32)
    mean = jnp.sum(values, axis=0) / total
    square = jnp.sum(values * values, axis=0) / total
    scales = lax.rsqrt(square - mean * mean + 1e-05)
    return mean, scales


def gram(rows, whole):
    partial = lax.dot_general(
        rows, whole, (((1,), (1,)), ((), ())), preferred_element_type=jnp.float32
    ).astype(jnp.bfloat16)
    mine = lax.psum_scatter(partial, "feat", scatter_dimension=1, tiled=True)
    return lax.all_gather(mine, "feat", axis=1, tiled=True)


def backward(back, unit, scales, first_sum, second_sum, total):
    return (scales * (back - first_sum / total - unit * (second_sum / total))).astype(jnp.bfloat16)


def body(view_a, view_b):
    rows_dev, width = view_a.shape
    total = rows_dev * lax.axis_size("batch")
    all_a = lax.all_gather(view_a, "batch", axis=0, tiled=True)
    all_b = lax.all_gather(view_b, "batch", axis=0, tiled=True)
    mean_a, scales_a = normalize(all_a, total)
    mean_b, scales_b = normalize(all_b, total)
    whole_a = ((all_a.astype(jnp.float32) - mean_a) * scales_a).astype(jnp.bfloat16)
    whole_b = ((all_b.astype(jnp.float32) - mean_b) * scales_b).astype(jnp.bfloat16)
    unit_a = (view_a.astype(jnp.float32) - mean_a) * scales_a
    unit_b = (view_b.astype(jnp.float32) - mean_b) * scales_b
    normed_a = unit_a.astype(jnp.bfloat16)
    normed_b = unit_b.astype(jnp.bfloat16)
    gram_b = gram(normed_b, whole_b)
    gram_a = gram(normed_a, whole_a)
    same = jnp.sum(whole_a.astype(jnp.float32) * whole_b.astype(jnp.float32), axis=0) / total
    extra = (2.0 * (same - 1.0)).astype(jnp.bfloat16).astype(jnp.float32) - 2.0 * LAMBDA * same
    factor = 2.0 * LAMBDA / total
    back_a = factor * jnp.dot(
        gram_b, whole_a, preferred_element_type=jnp.float32
    ) + extra * normed_b.astype(jnp.float32)
    back_b = factor * jnp.dot(
        gram_a, whole_b, preferred_element_type=jnp.float32
    ) + extra * normed_a.astype(jnp.float32)
    first_a, second_a, first_b, second_b = lax.psum(
        (
            jnp.sum(back_a, axis=0),
            jnp.sum(back_a * unit_a, axis=0),
            jnp.sum(back_b, axis=0),
            jnp.sum(back_b * unit_b, axis=0),
        ),
        "batch",
    )
    grad_a = backward(back_a, unit_a, scales_a, first_a, second_a, total)
    grad_b = backward(back_b, unit_b, scales_b, first_b, second_b, total)
    return (grad_a, grad_b)


def solution(mesh):
    return jax.shard_map(
        body,
        mesh=mesh,
        in_specs=(P("batch", "feat"), P("batch", "feat")),
        out_specs=(P("batch", "feat"), P("batch", "feat")),
        check_vma=False,
    )
```

```python
import functools

import jax
import jax.numpy as jnp
from jax import lax
from jax.experimental import pallas as pl
from jax.experimental.pallas import tpu as pltpu
from jax.sharding import PartitionSpec as P

LAMBDA = 0.0051
MESH = pl.DeviceIdType.MESH
F32 = jnp.float32
BF16 = jnp.bfloat16
COPIES = 256
REDUCED = (1024, 1024, 512)
GATHERED = (1024, 2048, 1024)


def rem4(value):
    return lax.rem(value, 4)


class Net:
    def __init__(self, send_sems, recv_sems):
        self.send_sems, self.recv_sems, self.copies = send_sems, recv_sems, []

    def copy(self, src, dst, device):
        n = len(self.copies)
        item = pltpu.make_async_remote_copy(
            src_ref=src,
            dst_ref=dst,
            send_sem=self.send_sems.at[n],
            recv_sem=self.recv_sems.at[n],
            device_id=device,
            device_id_type=MESH,
        )
        item.start()
        self.copies.append(item)
        return item

    def finish(self):
        for item in self.copies:
            item.wait_send()


def kernel(rows, total, va, vb, ga, gb, *scratch):
    (raw, normed, stat, same, last_a, last_b, moments, acc, send_sems, recv_sems) = scratch[:10]
    blocks = scratch[10:]
    net = Net(send_sems, recv_sems)
    views = (va, vb)
    batch, feat = lax.axis_index("batch"), lax.axis_index("feat")
    x, core = batch // 2, lax.rem(batch, 2)
    y, z = feat // 4, rem4(feat)

    def at_batch(dx, dcore):
        return (rem4(x + dx) * 2 + lax.rem(core + dcore, 2), feat)

    def at_feat(half, d1, d2):
        dy, dz = (d1, d2) if half == 0 else (d2, d1)
        return (batch, rem4(y + dy) * 4 + rem4(z + dz))

    peers = [(lax.rem(batch + k, 8), feat) for k in range(1, 8)]
    planes = [at_feat(half, k, 0) for half in range(2) for k in range(1, 4)]
    barrier = pltpu.get_barrier_semaphore()
    for device in peers + planes:
        pl.semaphore_signal(barrier, inc=1, device_id=device, device_id_type=MESH)

    def sums(step, carry):
        out = []
        for v in range(2):
            values = views[v][pl.ds(pl.multiple_of(step * 64, 64), 64), :].astype(F32)
            out.append(carry[2 * v] + jnp.sum(values.reshape(8, 8, -1), axis=0))
            out.append(carry[2 * v + 1] + jnp.sum((values * values).reshape(8, 8, -1), axis=0))
        return tuple(out)

    zero = jnp.zeros((8, rows), F32)
    parts = lax.fori_loop(0, rows // 64, sums, (zero,) * 4)
    for k in range(4):
        stat[batch, pl.ds(k, 1), :] = jnp.sum(parts[k], axis=0, keepdims=True)
    stat[batch, pl.ds(4, 4), :] = jnp.zeros((4, rows), F32)

    pl.semaphore_wait(barrier, len(peers) + len(planes))

    def exchange(ref):
        return [net.copy(ref.at[batch], ref.at[batch], device) for device in peers]

    def collect(ref, items):
        for item in items:
            item.wait_recv()
        result = ref[0]
        for k in range(1, 8):
            result = result + ref[k]
        return result

    stat_items = exchange(stat)
    sibling = (batch + 1 - 2 * core, feat)
    to_sib = {}
    near = {}
    far = {}
    for v in (1, 0):
        to_sib[v, 0] = net.copy(views[v], raw.at[v, 1], sibling)
        if v == 1:
            near[v] = (
                net.copy(views[v], raw.at[v, 6], at_batch(1, 0)),
                net.copy(views[v], raw.at[v, 2], at_batch(3, 0)),
            )

    sum_all = collect(stat, stat_items)
    for v in range(2):
        mean = sum_all[2 * v : 2 * v + 1] / total
        square = sum_all[2 * v + 1 : 2 * v + 2] / total
        moments[pl.ds(2 * v, 1), :] = mean
        moments[pl.ds(2 * v + 1, 1), :] = lax.rsqrt(square - mean * mean + 1e-05)

    def normalize(v, slot):
        source = views[v] if slot == 0 else raw.at[v, slot]

        @pl.loop(0, rows // 64)
        def _(step):
            here = pl.ds(pl.multiple_of(step * 64, 64), 64)
            values = source[here, :].astype(F32)
            unit = (values - moments[pl.ds(2 * v, 1), :]) * moments[pl.ds(2 * v + 1, 1), :]
            normed[v, slot, here, :] = unit.astype(BF16)

    def own_rows(v):
        normalize(v, 0)
        to_sib[v, 0].wait_recv()
        normalize(v, 1)

    def near_rows(v):
        from_left, from_right = near[v]
        from_left.wait_recv()
        from_right.wait_recv()
        half = rows // 2
        first, second = pl.ds(0, half), pl.ds(half, half)
        far[v] = (
            net.copy(raw.at[v, 6, first], raw.at[v, 4, first], at_batch(1, 0)),
            net.copy(raw.at[v, 2, second], raw.at[v, 4, second], at_batch(3, 0)),
        )
        to_sib[v, 2] = net.copy(raw.at[v, 2], raw.at[v, 3], sibling)
        to_sib[v, 6] = net.copy(raw.at[v, 6], raw.at[v, 7], sibling)
        if v == 1:
            near[0] = (
                net.copy(views[0], raw.at[0, 6], at_batch(1, 0)),
                net.copy(views[0], raw.at[0, 2], at_batch(3, 0)),
            )
        normalize(v, 2)
        normalize(v, 6)
        for slot in (2, 6):
            to_sib[v, slot].wait_recv()
            normalize(v, slot + 1)

    def far_rows(v):
        for item in far[v]:
            item.wait_recv()
        to_sib[v, 4] = net.copy(raw.at[v, 4], raw.at[v, 5], sibling)
        normalize(v, 4)
        to_sib[v, 4].wait_recv()
        normalize(v, 5)

    turned = x // 2

    class Block:
        def __init__(self, v, kind):
            self.v, self.kind = v, kind
            base = (v * 3 + kind) * 7
            (self.part, self.r1r, self.r1l, self.r2r, self.r2l, self.r3, self.full) = blocks[
                base : base + 7
            ]
            self.columns = REDUCED[kind]

        def mine(self, half):
            return (y, z) if half == 0 else (z, y)

        def product(self):
            v = self.v
            if self.kind == 0:
                own_rows(v)
            elif self.kind == 1:
                near_rows(v)
            else:
                far_rows(v)

            @pl.loop(0, rows // 128)
            def _(step):
                left = normed[v, 0, pl.ds(pl.multiple_of(step * 128, 128), 128), :]
                if self.kind == 2:
                    right = normed[v, 4 + turned]
                else:
                    right = normed[v, pl.ds(2 * self.kind, 2)].reshape(2 * rows, rows)
                value = lax.dot_general(
                    left, right, (((1,), (1,)), ((), ())), preferred_element_type=F32
                )
                self.part[pl.ds(step * 8, 8)] = value.astype(BF16).reshape(8, 16, self.columns)

            self.one = []
            for half in range(2):
                m1, _ = self.mine(half)
                base = half * 16 + rem4(m1 + 2) * 4
                self.one.append(
                    (
                        net.copy(
                            self.part.at[pl.ds(base + 2, 2)],
                            self.r1r.at[half],
                            at_feat(half, 1, 0),
                        ),
                        net.copy(
                            self.part.at[pl.ds(base, 2)], self.r1l.at[half], at_feat(half, 3, 0)
                        ),
                    )
                )

        def pass_on(self):
            self.two = []
            for half in range(2):
                m1, _ = self.mine(half)
                right = half * 16 + rem4(m1 + 1) * 4
                left = half * 16 + rem4(m1 + 3) * 4
                from_left, from_right = self.one[half]
                from_left.wait_recv()
                here = pl.ds(right + 2, 2)
                self.part[here] = (
                    self.part[here].astype(F32) + self.r1r[half].astype(F32)
                ).astype(BF16)
                first = net.copy(
                    self.part.at[pl.ds(right, 4)], self.r2r.at[half], at_feat(half, 1, 0)
                )
                from_right.wait_recv()
                here = pl.ds(left, 2)
                self.part[here] = (
                    self.part[here].astype(F32) + self.r1l[half].astype(F32)
                ).astype(BF16)
                second = net.copy(
                    self.part.at[pl.ds(left, 4)], self.r2l.at[half], at_feat(half, 3, 0)
                )
                self.two.append((first, second))

        def turn(self):
            self.three = []
            for half in range(2):
                m1, m2 = self.mine(half)
                base = half * 16 + m1 * 4
                for item in self.two[half]:
                    item.wait_recv()
                here = pl.ds(base, 4)
                self.part[here] = (
                    self.part[here].astype(F32)
                    + self.r2r[half].astype(F32)
                    + self.r2l[half].astype(F32)
                ).astype(BF16)
                self.three.append(
                    [
                        net.copy(
                            self.part.at[base + rem4(m2 + k)],
                            self.r3.at[half, k - 1],
                            at_feat(half, 0, k),
                        )
                        for k in range(1, 4)
                    ]
                )

        def own(self, half):
            m1, m2 = self.mine(half)
            return half * 16 + m1 * 4 + m2

        def reduced(self):
            self.mirror = []
            for half in range(2):
                for item in self.three[half]:
                    item.wait_recv()
                own = self.own(half)
                value = self.part[own].astype(F32)
                for k in range(3):
                    value = value + self.r3[half, k].astype(F32)
                self.full[own, :, pl.ds(0, self.columns)] = value.astype(BF16)
                if self.kind == 1:
                    for k in range(2):
                        self.mirror.append(
                            net.copy(
                                self.full.at[own, :, pl.ds(512 * k, 512)],
                                self.full.at[own, :, pl.ds(1024 + 512 * k, 512)],
                                at_batch(1, k),
                            )
                        )
                if self.kind == 2:
                    self.mirror.append(
                        net.copy(
                            self.full.at[own, :, pl.ds(0, 512)],
                            self.full.at[own, :, pl.ds(512, 512)],
                            at_batch(2, turned),
                        )
                    )
            if self.kind == 0:
                self.spread()

        def spread(self):
            for item in self.mirror:
                item.wait_recv()
            self.four = []
            for half in range(2):
                own = self.own(half)
                self.four.append(
                    [
                        net.copy(self.full.at[own], self.full.at[own], at_feat(half, 0, k))
                        for k in range(1, 4)
                    ]
                )

        def gather(self):
            self.five = []
            for half in range(2):
                m1, _ = self.mine(half)
                for item in self.four[half]:
                    item.wait_recv()
                here = self.full.at[pl.ds(half * 16 + m1 * 4, 4)]
                self.five.append(
                    (
                        net.copy(here, here, at_feat(half, 1, 0)),
                        net.copy(here, here, at_feat(half, 3, 0)),
                    )
                )

        def gather_on(self):
            self.six = []
            for half in range(2):
                m1, _ = self.mine(half)
                from_left, from_right = self.five[half]
                from_left.wait_recv()
                here = self.full.at[pl.ds(half * 16 + rem4(m1 + 3) * 4, 2)]
                first = net.copy(here, here, at_feat(half, 1, 0))
                from_right.wait_recv()
                here = self.full.at[pl.ds(half * 16 + rem4(m1 + 1) * 4 + 2, 2)]
                second = net.copy(here, here, at_feat(half, 3, 0))
                self.six.append((first, second))

        def apply(self):
            for half in range(2):
                for item in self.six[half]:
                    item.wait_recv()
            v, other = self.v, 1 - self.v

            @pl.loop(0, rows // 128)
            def _(step):
                here = pl.ds(pl.multiple_of(step * 128, 128), 128)
                left = self.full[pl.ds(step * 8, 8), :, pl.ds(0, self.columns)].reshape(
                    128, self.columns
                )
                if self.kind == 2:
                    right = normed[other, 4 + turned]
                else:
                    right = normed[other, pl.ds(2 * self.kind, 2)].reshape(2 * rows, rows)
                value = jnp.dot(left, right, preferred_element_type=F32)
                for k in range(GATHERED[self.kind] // 512 - self.columns // 512):
                    start = pl.multiple_of(self.columns + 512 * k + step * 128, 128)
                    left = self.full[:, :, pl.ds(start, 128)].reshape(rows, 128)
                    slot = 6 + k if self.kind == 1 else 5 - turned
                    value = value + lax.dot_general(
                        left,
                        normed[other, slot],
                        (((0,), (0,)), ((), ())),
                        preferred_element_type=F32,
                    )
                if self.kind == 0:
                    acc[other, here, :] = value
                else:
                    acc[other, here, :] = acc[other, here, :] + value

        def stages(self):
            steps = [self.product, self.pass_on, self.turn, self.reduced]
            if self.kind != 0:
                steps.append(self.spread)
            return steps + [self.gather, self.gather_on, self.apply]

    same_items = []

    def diagonal():
        def step_sum(step, carry):
            here = pl.ds(pl.multiple_of(step * 64, 64), 64)
            both = normed[0, 0, here, :].astype(F32) * normed[1, 0, here, :].astype(F32)
            return carry + jnp.sum(both.reshape(8, 8, -1), axis=0)

        part = lax.fori_loop(0, rows // 64, step_sum, zero)
        same[batch] = part
        same_items.extend(exchange(same))

    start = {(1, 0): 0, (0, 0): 1, (1, 1): 2, (1, 2): 3, (0, 1): 5, (0, 2): 6}
    running = [(begin, Block(v, kind)) for (v, kind), begin in start.items()]
    for tick in range(16):
        for begin, block in running:
            steps = block.stages()
            if 0 <= tick - begin < len(steps):
                steps[tick - begin]()
        if tick == 1:
            diagonal()

    cosine = jnp.sum(collect(same, same_items), axis=0, keepdims=True) / total
    extra = (2.0 * (cosine - 1.0)).astype(BF16).astype(F32) - 2.0 * LAMBDA * cosine
    factor = 2.0 * LAMBDA / total

    def unit_of(v, here):
        values = views[v][here, :].astype(F32)
        return (values - moments[pl.ds(2 * v, 1), :]) * moments[pl.ds(2 * v + 1, 1), :]

    def back_sums(v, last):
        def step_sum(step, carry):
            here = pl.ds(pl.multiple_of(step * 64, 64), 64)
            back = factor * acc[v, here, :] + extra * normed[1 - v, 0, here, :].astype(F32)
            acc[v, here, :] = back
            first = carry[0] + jnp.sum(back.reshape(8, 8, -1), axis=0)
            second = carry[1] + jnp.sum((back * unit_of(v, here)).reshape(8, 8, -1), axis=0)
            return first, second

        first, second = lax.fori_loop(0, rows // 64, step_sum, (zero, zero))
        last[batch, pl.ds(0, 1), :] = jnp.sum(first, axis=0, keepdims=True)
        last[batch, pl.ds(1, 1), :] = jnp.sum(second, axis=0, keepdims=True)
        last[batch, pl.ds(2, 6), :] = jnp.zeros((6, rows), F32)
        return exchange(last)

    def finish(v, last, items, out):
        both = collect(last, items) / total
        first, second = both[0:1], both[1:2]

        @pl.loop(0, rows // 64)
        def _(step):
            here = pl.ds(pl.multiple_of(step * 64, 64), 64)
            scale = moments[pl.ds(2 * v + 1, 1), :]
            value = scale * (acc[v, here, :] - first - unit_of(v, here) * second)
            out[here, :] = value.astype(BF16)

    items_a = back_sums(0, last_a)
    items_b = back_sums(1, last_b)
    finish(0, last_a, items_a, ga)
    finish(1, last_b, items_b, gb)
    net.finish()


def body(view_a, view_b):
    rows, width = view_a.shape
    total = rows * lax.axis_size("batch")
    blocks = []
    for _ in range(2):
        for columns, wide in zip(REDUCED, GATHERED):
            blocks += [
                pltpu.VMEM((32, 16, columns), BF16),
                pltpu.VMEM((2, 2, 16, columns), BF16),
                pltpu.VMEM((2, 2, 16, columns), BF16),
                pltpu.VMEM((2, 4, 16, columns), BF16),
                pltpu.VMEM((2, 4, 16, columns), BF16),
                pltpu.VMEM((2, 3, 16, columns), BF16),
                pltpu.VMEM((32, 16, wide), BF16),
            ]
    vmem = pl.BlockSpec(memory_space=pltpu.VMEM)
    return pl.pallas_call(
        functools.partial(kernel, rows, total),
        out_shape=(jax.ShapeDtypeStruct((rows, width), BF16),) * 2,
        in_specs=[vmem, vmem],
        out_specs=(vmem, vmem),
        scratch_shapes=[
            pltpu.VMEM((2, 8, rows, width), BF16),
            pltpu.VMEM((2, 8, rows, width), BF16),
            pltpu.VMEM((8, 8, width), F32),
            pltpu.VMEM((8, 8, width), F32),
            pltpu.VMEM((8, 8, width), F32),
            pltpu.VMEM((8, 8, width), F32),
            pltpu.VMEM((8, width), F32),
            pltpu.VMEM((2, rows, width), F32),
            pltpu.SemaphoreType.DMA((COPIES,)),
            pltpu.SemaphoreType.DMA((COPIES,)),
        ]
        + blocks,
        compiler_params=pltpu.CompilerParams(
            collective_id=0, has_side_effects=True, vmem_limit_bytes=56 * 2**20
        ),
        name="gram_gradient",
    )(view_a, view_b)


def solution(mesh):
    return jax.shard_map(
        body,
        mesh=mesh,
        in_specs=(P("batch", "feat"), P("batch", "feat")),
        out_specs=(P("batch", "feat"), P("batch", "feat")),
        check_vma=False,
    )
```

```python
import functools

import jax
import jax.numpy as jnp
from jax import lax
from jax.experimental import pallas as pl
from jax.experimental.pallas import tpu as pltpu
from jax.sharding import PartitionSpec as P

LAMBDA = 0.0051
MESH = pl.DeviceIdType.MESH
F32 = jnp.float32
BF16 = jnp.bfloat16
SENDS, RECEIVES = 20, 60
REDUCED = (768, 1024, 512)
GATHERED = (768, 2048, 1024)


def rem4(value):
    return lax.rem(value, 4)


class Net:
    def __init__(self, send_sems, recv_sems):
        self.send_sems, self.recv_sems = send_sems, recv_sems
        self.sends, self.receives = [], 0

    def sender(self, moved):
        self.sends.append(moved)
        return self.send_sems.at[len(self.sends) - 1]

    def receiver(self):
        self.receives += 1
        return self.recv_sems.at[self.receives - 1]

    def finish(self):
        for n, moved in enumerate(self.sends):
            wait(self.send_sems.at[n], moved)


def send(src, dst, sender, receiver, device):
    pltpu.make_async_remote_copy(
        src_ref=src,
        dst_ref=dst,
        send_sem=sender,
        recv_sem=receiver,
        device_id=device,
        device_id_type=MESH,
    ).start()


def wait(sem, moved):
    pltpu.make_async_copy(moved, moved, sem).wait()


def kernel(rows, total, va, vb, ga, gb, *scratch):
    (raw, normed, stat, same, last_a, last_b, moments, acc, cross, send_sems, recv_sems) = scratch[:11]
    blocks = scratch[11:]
    net = Net(send_sems, recv_sems)
    views = (va, vb)
    batch, feat = lax.axis_index("batch"), lax.axis_index("feat")
    x, core = batch // 2, lax.rem(batch, 2)
    y, z = feat // 4, rem4(feat)

    def at_batch(dx, dcore):
        return (rem4(x + dx) * 2 + lax.rem(core + dcore, 2), feat)

    def at_feat(half, d1, d2):
        dy, dz = (d1, d2) if half == 0 else (d2, d1)
        return (batch, rem4(y + dy) * 4 + rem4(z + dz))

    peers = [(lax.rem(batch + k, 8), feat) for k in range(1, 8)]
    planes = [at_feat(half, k, 0) for half in range(2) for k in range(1, 4)]
    barrier = pltpu.get_barrier_semaphore()
    for device in peers + planes:
        pl.semaphore_signal(barrier, inc=1, device_id=device, device_id_type=MESH)

    def sums(step, carry):
        out = []
        for v in range(2):
            values = views[v][pl.ds(pl.multiple_of(step * 64, 64), 64), :].astype(F32)
            out.append(carry[2 * v] + jnp.sum(values.reshape(8, 8, -1), axis=0))
            out.append(carry[2 * v + 1] + jnp.sum((values * values).reshape(8, 8, -1), axis=0))
        return tuple(out)

    zero = jnp.zeros((8, rows), F32)
    parts = lax.fori_loop(0, rows // 64, sums, (zero,) * 4)
    for k in range(4):
        stat[batch, pl.ds(k, 1), :] = jnp.sum(parts[k], axis=0, keepdims=True)
    stat[batch, pl.ds(4, 4), :] = jnp.zeros((4, rows), F32)

    pl.semaphore_wait(barrier, len(peers) + len(planes))

    def exchange(ref):
        sender, receiver = net.sender(ref.at[pl.ds(0, 7)]), net.receiver()
        for device in peers:
            send(ref.at[batch], ref.at[batch], sender, receiver, device)
        return receiver

    def collect(ref, receiver):
        wait(receiver, ref.at[pl.ds(0, 7)])
        result = ref[0]
        for k in range(1, 8):
            result = result + ref[k]
        return result

    stat_items = exchange(stat)
    sibling = (batch + 1 - 2 * core, feat)
    half = rows // 2
    upper, lower = pl.ds(0, half), pl.ds(half, half)
    view_sends = [net.sender(raw.at[v, pl.ds(0, 7)]) for v in range(2)]
    view_sems = [[net.receiver() for _ in range(7)] for _ in range(2)]

    def send_rows(v, src, slot, device, part=None):
        dst = raw.at[v, slot] if part is None else raw.at[v, slot, part]
        send(src, dst, view_sends[v], view_sems[v][slot - 1], device)

    def wait_rows(v, slot):
        wait(view_sems[v][slot - 1], raw.at[v, slot])

    def send_near(v):
        send_rows(v, views[v], 6, at_batch(1, 0))
        send_rows(v, views[v], 2, at_batch(3, 0))

    send_near(1)
    for v in (1, 0):
        send_rows(v, views[v], 1, sibling)

    sum_all = collect(stat, stat_items)
    for v in range(2):
        mean = sum_all[2 * v : 2 * v + 1] / total
        square = sum_all[2 * v + 1 : 2 * v + 2] / total
        moments[pl.ds(2 * v, 1), :] = mean
        moments[pl.ds(2 * v + 1, 1), :] = lax.rsqrt(square - mean * mean + 1e-05)

    def normalize(v, slot):
        source = views[v] if slot == 0 else raw.at[v, slot]

        @pl.loop(0, rows // 64)
        def _(step):
            here = pl.ds(pl.multiple_of(step * 64, 64), 64)
            values = source[here, :].astype(F32)
            unit = (values - moments[pl.ds(2 * v, 1), :]) * moments[pl.ds(2 * v + 1, 1), :]
            normed[v, slot, here, :] = unit.astype(BF16)

    def own_rows(v):
        normalize(v, 0)
        wait_rows(v, 1)
        normalize(v, 1)

    def near_rows(v):
        wait_rows(v, 6)
        wait_rows(v, 2)
        send_rows(v, raw.at[v, 6, upper], 4, at_batch(1, 0), upper)
        send_rows(v, raw.at[v, 2, lower], 4, at_batch(3, 0), lower)
        send_rows(v, raw.at[v, 2], 3, sibling)
        send_rows(v, raw.at[v, 6], 7, sibling)
        if v == 1:
            send_near(0)
        normalize(v, 2)
        normalize(v, 6)
        for slot in (3, 7):
            wait_rows(v, slot)
            normalize(v, slot)

    def far_rows(v):
        wait_rows(v, 4)
        send_rows(v, raw.at[v, 4], 5, sibling)
        normalize(v, 4)
        wait_rows(v, 5)
        normalize(v, 5)

    net.cross_sends = [net.sender(cross.at[v]) for v in range(2)]

    def cross_rows(part, turn):
        return pl.ds(pl.multiple_of(lax.rem(part + turn, 2) * 256, 256), 256)

    turned = x // 2

    class Block:
        def __init__(self, v, kind):
            self.v, self.kind = v, kind
            base = (v * 3 + kind) * 5
            self.part, self.r1, self.r2, self.r3, self.full = blocks[base : base + 5]
            self.cross = cross.at[v]
            self.columns = REDUCED[kind]
            mirrored = 0 if kind == 0 else 1
            self.reduce_send = net.sender(self.part.at[pl.ds(0, 30)])
            self.gather_send = net.sender(self.full.at[pl.ds(0, 30 + mirrored)])
            self.sems = [net.receiver() for _ in range(7)]

        def mine(self, half):
            return (y, z) if half == 0 else (z, y)

        def product(self):
            v = self.v
            if self.kind == 0:
                own_rows(v)
            elif self.kind == 1:
                near_rows(v)
            else:
                far_rows(v)

            @pl.loop(0, rows // 128)
            def _(step):
                left = normed[v, 0, pl.ds(pl.multiple_of(step * 128, 128), 128), :]

                def block(first, right):
                    value = lax.dot_general(
                        left, right, (((1,), (1,)), ((), ())), preferred_element_type=F32
                    )
                    width = right.shape[0]
                    self.part[pl.ds(step * 8, 8), :, pl.ds(first, width)] = value.astype(
                        BF16
                    ).reshape(8, 16, width)

                if self.kind == 0:
                    block(0, normed[v, 0])
                    block(rows, normed[v, 1, cross_rows(step // 2, core), :])
                elif self.kind == 1:
                    block(0, normed[v, pl.ds(2, 2)].reshape(2 * rows, rows))
                else:
                    block(0, normed[v, 4 + turned])

            for half in range(2):
                m1, _ = self.mine(half)
                base = half * 16 + rem4(m1 + 2) * 4
                for k in range(2):
                    send(
                        self.part.at[pl.ds(base + 2 * (1 - k), 2)],
                        self.r1.at[half, k],
                        self.reduce_send,
                        self.sems[0],
                        at_feat(half, 1 + 2 * k, 0),
                    )

        def pass_on(self):
            wait(self.sems[0], self.r1)
            for half in range(2):
                m1, _ = self.mine(half)
                for k in range(2):
                    base = half * 16 + rem4(m1 + 1 + 2 * k) * 4
                    here = pl.ds(base + 2 * (1 - k), 2)
                    self.part[here] = (
                        self.part[here].astype(F32) + self.r1[half, k].astype(F32)
                    ).astype(BF16)
                    send(
                        self.part.at[pl.ds(base, 4)],
                        self.r2.at[half, k],
                        self.reduce_send,
                        self.sems[1],
                        at_feat(half, 1 + 2 * k, 0),
                    )

        def turn(self):
            wait(self.sems[1], self.r2)
            for half in range(2):
                m1, m2 = self.mine(half)
                base = half * 16 + m1 * 4
                here = pl.ds(base, 4)
                self.part[here] = (
                    self.part[here].astype(F32)
                    + self.r2[half, 0].astype(F32)
                    + self.r2[half, 1].astype(F32)
                ).astype(BF16)
                for k in range(1, 4):
                    send(
                        self.part.at[base + rem4(m2 + k)],
                        self.r3.at[half, k - 1],
                        self.reduce_send,
                        self.sems[2],
                        at_feat(half, 0, k),
                    )

        def own(self, half):
            m1, m2 = self.mine(half)
            return half * 16 + m1 * 4 + m2

        def mirror(self, own, first, start, device):
            send(
                self.full.at[own, :, pl.ds(first, 512)],
                self.full.at[own, :, pl.ds(start, 512)],
                self.gather_send,
                self.sems[3],
                device,
            )

        def reduced(self):
            wait(self.sems[2], self.r3)
            for half in range(2):
                own = self.own(half)
                value = self.part[own].astype(F32)
                for k in range(3):
                    value = value + self.r3[half, k].astype(F32)
                self.full[own, :, pl.ds(0, self.columns)] = value.astype(BF16)
                if self.kind == 1:
                    for k in range(2):
                        self.mirror(own, 512 * k, 1024 + 512 * k, at_batch(1, k))
                if self.kind == 2:
                    self.mirror(own, 0, 512, at_batch(2, turned))
            if self.kind == 0:
                self.spread()

        def spread(self):
            if self.kind != 0:
                wait(self.sems[3], self.full.at[pl.ds(0, 1)])
            for half in range(2):
                here = self.full.at[self.own(half)]
                for k in range(1, 4):
                    send(here, here, self.gather_send, self.sems[4], at_feat(half, 0, k))

        def gather(self):
            wait(self.sems[4], self.full.at[pl.ds(0, 6)])
            for half in range(2):
                m1, _ = self.mine(half)
                here = self.full.at[pl.ds(half * 16 + m1 * 4, 4)]
                for k in range(2):
                    send(here, here, self.gather_send, self.sems[5], at_feat(half, 1 + 2 * k, 0))

        def gather_on(self):
            wait(self.sems[5], self.full.at[pl.ds(0, 16)])
            for half in range(2):
                m1, _ = self.mine(half)
                for k in range(2):
                    base = half * 16 + rem4(m1 + 3 + 2 * k) * 4
                    here = self.full.at[pl.ds(base + 2 * k, 2)]
                    send(here, here, self.gather_send, self.sems[6], at_feat(half, 1 + 2 * k, 0))

        def arrived(self):
            wait(self.sems[6], self.full.at[pl.ds(0, 8)])

        def swap(self):
            self.arrived()
            send(
                self.full.at[:, :, pl.ds(rows, rows // 2)],
                self.cross,
                net.cross_sends[self.v],
                self.sems[3],
                sibling,
            )

        def apply(self):
            if self.kind == 0:
                wait(self.sems[3], self.cross)
            else:
                self.arrived()
            other = 1 - self.v

            @pl.loop(0, rows // 128)
            def _(step):
                here = pl.ds(pl.multiple_of(step * 128, 128), 128)

                def direct(first, right):
                    width = right.shape[0]
                    left = self.full[pl.ds(step * 8, 8), :, pl.ds(first, width)]
                    return jnp.dot(
                        left.reshape(128, width), right, preferred_element_type=F32
                    )

                def mirrored(left, right):
                    return lax.dot_general(
                        left.reshape(-1, 128),
                        right,
                        (((0,), (0,)), ((), ())),
                        preferred_element_type=F32,
                    )

                def columns(first):
                    return pl.ds(pl.multiple_of(first + step * 128, 128), 128)

                if self.kind == 0:
                    value = direct(0, normed[other, 0])
                    value += direct(rows, normed[other, 1, cross_rows(step // 2, core), :])
                    theirs = lax.rem(step // 2 + 1 - core, 2)
                    first = pl.multiple_of(lax.rem(step, 2) * 128, 128)
                    left = self.cross[pl.ds(theirs * 16, 16), :, pl.ds(first, 128)]
                    value += mirrored(left, normed[other, 1, cross_rows(theirs, 0), :])
                    acc[other, here, :] = value
                elif self.kind == 1:
                    value = direct(0, normed[other, pl.ds(2, 2)].reshape(2 * rows, rows))
                    for k in range(2):
                        left = self.full[:, :, columns(1024 + 512 * k)]
                        value += mirrored(left, normed[other, 6 + k])
                    acc[other, here, :] += value
                else:
                    value = direct(0, normed[other, 4 + turned])
                    left = self.full[:, :, columns(512)]
                    value += mirrored(left, normed[other, 5 - turned])
                    acc[other, here, :] += value

        def stages(self):
            steps = [self.product, self.pass_on, self.turn, self.reduced]
            if self.kind != 0:
                steps.append(self.spread)
            steps += [self.gather, self.gather_on]
            if self.kind == 0:
                steps.append(self.swap)
            return steps + [self.apply]

    same_items = []

    def diagonal():
        def step_sum(step, carry):
            here = pl.ds(pl.multiple_of(step * 64, 64), 64)
            both = normed[0, 0, here, :].astype(F32) * normed[1, 0, here, :].astype(F32)
            return carry + jnp.sum(both.reshape(8, 8, -1), axis=0)

        part = lax.fori_loop(0, rows // 64, step_sum, zero)
        same[batch] = part
        same_items.append(exchange(same))

    def unit_of(v, here):
        values = views[v][here, :].astype(F32)
        return (values - moments[pl.ds(2 * v, 1), :]) * moments[pl.ds(2 * v + 1, 1), :]

    def back_sums(v, last):
        def step_sum(step, carry):
            here = pl.ds(pl.multiple_of(step * 64, 64), 64)
            back = (2.0 * LAMBDA / total) * acc[v, here, :]
            back += extra * normed[1 - v, 0, here, :].astype(F32)
            acc[v, here, :] = back
            first = carry[0] + jnp.sum(back.reshape(8, 8, -1), axis=0)
            second = carry[1] + jnp.sum((back * unit_of(v, here)).reshape(8, 8, -1), axis=0)
            return first, second

        first, second = lax.fori_loop(0, rows // 64, step_sum, (zero, zero))
        last[batch, pl.ds(0, 1), :] = jnp.sum(first, axis=0, keepdims=True)
        last[batch, pl.ds(1, 1), :] = jnp.sum(second, axis=0, keepdims=True)
        last[batch, pl.ds(2, 6), :] = jnp.zeros((6, rows), F32)
        return exchange(last)

    def finish(v, last, items, out):
        both = collect(last, items) / total
        first, second = both[0:1], both[1:2]

        @pl.loop(0, rows // 64)
        def _(step):
            here = pl.ds(pl.multiple_of(step * 64, 64), 64)
            scale = moments[pl.ds(2 * v + 1, 1), :]
            value = scale * (acc[v, here, :] - first - unit_of(v, here) * second)
            out[here, :] = value.astype(BF16)

    start = {(1, 0): 0, (0, 0): 1, (1, 1): 2, (1, 2): 3, (0, 1): 5, (0, 2): 6}
    running = [(begin, Block(v, kind)) for (v, kind), begin in start.items()]
    ends = {(block.v, block.kind): begin + len(block.stages()) - 1 for begin, block in running}
    early = max(end for (v, _), end in ends.items() if v == 1)
    for tick in range(max(ends.values()) + 1):
        for begin, block in running:
            steps = block.stages()
            if 0 <= tick - begin < len(steps):
                steps[tick - begin]()
        if tick == 1:
            diagonal()
        if tick == early:
            cosine = jnp.sum(collect(same, same_items[0]), axis=0, keepdims=True) / total
            extra = (2.0 * (cosine - 1.0)).astype(BF16).astype(F32) - 2.0 * LAMBDA * cosine
            items_a = back_sums(0, last_a)
    items_b = back_sums(1, last_b)
    finish(0, last_a, items_a, ga)
    finish(1, last_b, items_b, gb)
    net.finish()
    assert (len(net.sends), net.receives) == (SENDS, RECEIVES)


def body(view_a, view_b):
    rows, width = view_a.shape
    total = rows * lax.axis_size("batch")
    blocks = []
    for _ in range(2):
        for columns, wide in zip(REDUCED, GATHERED):
            blocks += [
                pltpu.VMEM((32, 16, columns), BF16),
                pltpu.VMEM((2, 2, 2, 16, columns), BF16),
                pltpu.VMEM((2, 2, 4, 16, columns), BF16),
                pltpu.VMEM((2, 3, 16, columns), BF16),
                pltpu.VMEM((32, 16, wide), BF16),
            ]
    vmem = pl.BlockSpec(memory_space=pltpu.VMEM)
    return pl.pallas_call(
        functools.partial(kernel, rows, total),
        out_shape=(jax.ShapeDtypeStruct((rows, width), BF16),) * 2,
        in_specs=[vmem, vmem],
        out_specs=(vmem, vmem),
        scratch_shapes=[
            pltpu.VMEM((2, 8, rows, width), BF16),
            pltpu.VMEM((2, 8, rows, width), BF16),
            pltpu.VMEM((8, 8, width), F32),
            pltpu.VMEM((8, 8, width), F32),
            pltpu.VMEM((8, 8, width), F32),
            pltpu.VMEM((8, 8, width), F32),
            pltpu.VMEM((8, width), F32),
            pltpu.VMEM((2, rows, width), F32),
            pltpu.VMEM((2, 32, 16, 256), BF16),
            pltpu.SemaphoreType.DMA((SENDS,)),
            pltpu.SemaphoreType.DMA((RECEIVES,)),
        ]
        + blocks,
        compiler_params=pltpu.CompilerParams(
            collective_id=0, has_side_effects=True, vmem_limit_bytes=56 * 2**20
        ),
        name="gram_gradient",
    )(view_a, view_b)


def solution(mesh):
    return jax.shard_map(
        body,
        mesh=mesh,
        in_specs=(P("batch", "feat"), P("batch", "feat")),
        out_specs=(P("batch", "feat"), P("batch", "feat")),
        check_vma=False,
    )
```

```python
import functools

import jax
import jax.numpy as jnp
from jax import lax
from jax.experimental import pallas as pl
from jax.experimental.pallas import tpu as pltpu
from jax.sharding import PartitionSpec as P

LAMBDA = 0.0051
MESH = pl.DeviceIdType.MESH
F32 = jnp.float32
BF16 = jnp.bfloat16
SENDS, RECEIVES = 22, 60
REDUCED = (768, 1024, 512)
GATHERED = (768, 1024, 1024)
ROWS = ((0, 1), (3,), (6, 8, 11, 15), (21, 24, 29, 31))
BLOCKS = (
    (1, 0, (4, 7, 12, 16, 23, 40, 49, 53)),
    (0, 0, (2, 5, 9, 13, 19, 45, 48, 56)),
    (1, 1, (10, 14, 18, 22, 27, 36, 43, 50)),
    (1, 2, (17, 20, 26, 30, 33, 39, 51, 55)),
    (0, 1, (25, 28, 34, 37, 42, 46, 52, 57)),
    (0, 2, (32, 35, 38, 41, 44, 47, 54, 58)),
)


def rem4(value):
    return lax.rem(value, 4)


class Net:
    def __init__(self, send_sems, recv_sems):
        self.send_sems, self.recv_sems = send_sems, recv_sems
        self.sends, self.receives = [], 0

    def sender(self, moved):
        self.sends.append(moved)
        return self.send_sems.at[len(self.sends) - 1]

    def receiver(self):
        self.receives += 1
        return self.recv_sems.at[self.receives - 1]

    def finish(self):
        for n, moved in enumerate(self.sends):
            wait(self.send_sems.at[n], moved)


def send(src, dst, sender, receiver, device):
    pltpu.make_async_remote_copy(
        src_ref=src,
        dst_ref=dst,
        send_sem=sender,
        recv_sem=receiver,
        device_id=device,
        device_id_type=MESH,
    ).start()


def wait(sem, moved):
    pltpu.make_async_copy(moved, moved, sem).wait()


def kernel(rows, total, va, vb, ga, gb, *scratch):
    (raw, normed, stat, same, last_a, last_b, moments, acc, cross, back, send_sems, recv_sems) = scratch[:12]
    blocks = scratch[12:]
    net = Net(send_sems, recv_sems)
    views = (va, vb)
    batch, feat = lax.axis_index("batch"), lax.axis_index("feat")
    x, core = batch // 2, lax.rem(batch, 2)
    y, z = feat // 4, rem4(feat)

    def at_batch(dx, dcore):
        return (rem4(x + dx) * 2 + lax.rem(core + dcore, 2), feat)

    def at_feat(half, d1, d2):
        dy, dz = (d1, d2) if half == 0 else (d2, d1)
        return (batch, rem4(y + dy) * 4 + rem4(z + dz))

    peers = [(lax.rem(batch + k, 8), feat) for k in range(1, 8)]
    planes = [at_feat(half, k, 0) for half in range(2) for k in range(1, 4)]
    barrier = pltpu.get_barrier_semaphore()
    for device in peers + planes:
        pl.semaphore_signal(barrier, inc=1, device_id=device, device_id_type=MESH)

    def sums(step, carry):
        out = []
        for v in range(2):
            values = views[v][pl.ds(pl.multiple_of(step * 64, 64), 64), :].astype(F32)
            out.append(carry[2 * v] + jnp.sum(values.reshape(8, 8, -1), axis=0))
            out.append(carry[2 * v + 1] + jnp.sum((values * values).reshape(8, 8, -1), axis=0))
        return tuple(out)

    zero = jnp.zeros((8, rows), F32)
    parts = lax.fori_loop(0, rows // 64, sums, (zero,) * 4)
    for k in range(4):
        stat[batch, pl.ds(k, 1), :] = jnp.sum(parts[k], axis=0, keepdims=True)
    stat[batch, pl.ds(4, 4), :] = jnp.zeros((4, rows), F32)

    pl.semaphore_wait(barrier, len(peers) + len(planes))

    def exchange(ref):
        sender, receiver = net.sender(ref.at[pl.ds(0, 7)]), net.receiver()
        for device in peers:
            send(ref.at[batch], ref.at[batch], sender, receiver, device)
        return receiver

    def collect(ref, receiver):
        wait(receiver, ref.at[pl.ds(0, 7)])
        result = ref[0]
        for k in range(1, 8):
            result = result + ref[k]
        return result

    stat_items = exchange(stat)
    sibling = (batch + 1 - 2 * core, feat)
    half = rows // 2
    upper, lower = pl.ds(0, half), pl.ds(half, half)
    view_sends = [net.sender(raw.at[v, pl.ds(0, 7)]) for v in range(2)]
    view_sems = [[net.receiver() for _ in range(7)] for _ in range(2)]

    def send_rows(v, src, slot, device, part=None):
        dst = raw.at[v, slot] if part is None else raw.at[v, slot, part]
        send(src, dst, view_sends[v], view_sems[v][slot - 1], device)

    def wait_rows(v, slot):
        wait(view_sems[v][slot - 1], raw.at[v, slot])

    def send_near(v):
        send_rows(v, views[v], 6, at_batch(1, 0))
        send_rows(v, views[v], 2, at_batch(3, 0))

    send_near(1)
    for v in (1, 0):
        send_rows(v, views[v], 1, sibling)

    sum_all = collect(stat, stat_items)
    for v in range(2):
        mean = sum_all[2 * v : 2 * v + 1] / total
        square = sum_all[2 * v + 1 : 2 * v + 2] / total
        moments[pl.ds(2 * v, 1), :] = mean
        moments[pl.ds(2 * v + 1, 1), :] = lax.rsqrt(square - mean * mean + 1e-05)

    def normalize(v, slot):
        source = views[v] if slot == 0 else raw.at[v, slot]

        @pl.loop(0, rows // 64)
        def _(step):
            here = pl.ds(pl.multiple_of(step * 64, 64), 64)
            values = source[here, :].astype(F32)
            unit = (values - moments[pl.ds(2 * v, 1), :]) * moments[pl.ds(2 * v + 1, 1), :]
            normed[v, slot, here, :] = unit.astype(BF16)

    def own_rows(v):
        normalize(v, 0)
        wait_rows(v, 1)
        normalize(v, 1)

    def near_rows(v):
        wait_rows(v, 6)
        wait_rows(v, 2)
        send_rows(v, raw.at[v, 6, upper], 4, at_batch(1, 0), upper)
        send_rows(v, raw.at[v, 2, lower], 4, at_batch(3, 0), lower)
        send_rows(v, raw.at[v, 2], 3, sibling)
        send_rows(v, raw.at[v, 6], 7, sibling)
        if v == 1:
            send_near(0)

    def take_near(v):
        normalize(v, 2)
        normalize(v, 6)
        for slot in (3, 7):
            wait_rows(v, slot)
            normalize(v, slot)

    def far_rows(v):
        wait_rows(v, 4)
        send_rows(v, raw.at[v, 4], 5, sibling)

    def take_far(v):
        normalize(v, 4)
        wait_rows(v, 5)
        normalize(v, 5)

    net.cross_sends = [net.sender(cross.at[v]) for v in range(2)]
    net.back_sends = [net.sender(back.at[v]) for v in range(2)]
    begun = set()

    def cross_rows(part, turn):
        return pl.ds(pl.multiple_of(lax.rem(part + turn, 2) * 256, 256), 256)

    turned = x // 2

    def mirrored(left, right):
        return lax.dot_general(
            left.reshape(-1, 128), right, (((0,), (0,)), ((), ())), preferred_element_type=F32
        )

    def add(v, here, value):
        acc[v, here, :] = acc[v, here, :] + value if v in begun else value

    class Block:
        def __init__(self, v, kind):
            self.v, self.kind = v, kind
            base = (v * 3 + kind) * 5
            self.part, self.r1, self.r2, self.r3, self.full = blocks[base : base + 5]
            self.cross, self.back = cross.at[v], back.at[v]
            self.columns = REDUCED[kind]
            mirrored = 1 if kind == 2 else 0
            self.reduce_send = net.sender(self.part.at[pl.ds(0, 30)])
            self.gather_send = net.sender(self.full.at[pl.ds(0, 30 + mirrored)])
            self.sems = [net.receiver() for _ in range(7)]

        def mine(self, half):
            return (y, z) if half == 0 else (z, y)

        def product(self):
            v = self.v
            @pl.loop(0, rows // 128)
            def _(step):
                left = normed[v, 0, pl.ds(pl.multiple_of(step * 128, 128), 128), :]

                def block(first, right):
                    value = lax.dot_general(
                        left, right, (((1,), (1,)), ((), ())), preferred_element_type=F32
                    )
                    width = right.shape[0]
                    self.part[pl.ds(step * 8, 8), :, pl.ds(first, width)] = value.astype(
                        BF16
                    ).reshape(8, 16, width)

                if self.kind == 0:
                    block(0, normed[v, 0])
                    block(rows, normed[v, 1, cross_rows(step // 2, core), :])
                elif self.kind == 1:
                    block(0, normed[v, 2])
                    block(rows, normed[v, 7])
                else:
                    block(0, normed[v, 4 + turned])

            for half in range(2):
                m1, _ = self.mine(half)
                base = half * 16 + rem4(m1 + 2) * 4
                for k in range(2):
                    send(
                        self.part.at[pl.ds(base + 2 * (1 - k), 2)],
                        self.r1.at[half, k],
                        self.reduce_send,
                        self.sems[0],
                        at_feat(half, 1 + 2 * k, 0),
                    )

        def pass_on(self):
            wait(self.sems[0], self.r1)
            for half in range(2):
                m1, _ = self.mine(half)
                for k in range(2):
                    base = half * 16 + rem4(m1 + 1 + 2 * k) * 4
                    here = pl.ds(base + 2 * (1 - k), 2)
                    self.part[here] = (
                        self.part[here].astype(F32) + self.r1[half, k].astype(F32)
                    ).astype(BF16)
                    send(
                        self.part.at[pl.ds(base, 4)],
                        self.r2.at[half, k],
                        self.reduce_send,
                        self.sems[1],
                        at_feat(half, 1 + 2 * k, 0),
                    )

        def turn(self):
            wait(self.sems[1], self.r2)
            for half in range(2):
                m1, m2 = self.mine(half)
                base = half * 16 + m1 * 4
                here = pl.ds(base, 4)
                self.part[here] = (
                    self.part[here].astype(F32)
                    + self.r2[half, 0].astype(F32)
                    + self.r2[half, 1].astype(F32)
                ).astype(BF16)
                for k in range(1, 4):
                    send(
                        self.part.at[base + rem4(m2 + k)],
                        self.r3.at[half, k - 1],
                        self.reduce_send,
                        self.sems[2],
                        at_feat(half, 0, k),
                    )

        def own(self, half):
            m1, m2 = self.mine(half)
            return half * 16 + m1 * 4 + m2

        def mirror(self, own, first, start, device):
            send(
                self.full.at[own, :, pl.ds(first, 512)],
                self.full.at[own, :, pl.ds(start, 512)],
                self.gather_send,
                self.sems[3],
                device,
            )

        def reduced(self):
            wait(self.sems[2], self.r3)
            for half in range(2):
                own = self.own(half)
                value = self.part[own].astype(F32)
                for k in range(3):
                    value = value + self.r3[half, k].astype(F32)
                self.full[own, :, pl.ds(0, self.columns)] = value.astype(BF16)
                if self.kind == 2:
                    self.mirror(own, 0, 512, at_batch(2, turned))
            if self.kind != 2:
                self.spread()

        def spread(self):
            if self.kind == 2:
                wait(self.sems[3], self.full.at[pl.ds(0, 1)])
            for half in range(2):
                here = self.full.at[self.own(half)]
                for k in range(1, 4):
                    send(here, here, self.gather_send, self.sems[4], at_feat(half, 0, k))

        def send_back(self, half, ahead, first, count):
            m1, _ = self.mine(half)
            chunks = pl.ds(half * 16 + rem4(m1 + ahead) * 4 + first, count)
            for k, device in enumerate((at_batch(1, 0), at_batch(3, 1))):
                send(
                    self.full.at[chunks, :, pl.ds(512 * k, 512)],
                    self.back.at[k, chunks],
                    net.back_sends[self.v],
                    self.sems[3],
                    device,
                )

        def gather(self):
            wait(self.sems[4], self.full.at[pl.ds(0, 6)])
            for half in range(2):
                m1, _ = self.mine(half)
                here = self.full.at[pl.ds(half * 16 + m1 * 4, 4)]
                for k in range(2):
                    send(here, here, self.gather_send, self.sems[5], at_feat(half, 1 + 2 * k, 0))
                if self.kind == 1:
                    self.send_back(half, 0, 0, 4)

        def gather_on(self):
            wait(self.sems[5], self.full.at[pl.ds(0, 16)])
            for half in range(2):
                m1, _ = self.mine(half)
                for k in range(2):
                    base = half * 16 + rem4(m1 + 3 + 2 * k) * 4
                    here = self.full.at[pl.ds(base + 2 * k, 2)]
                    send(here, here, self.gather_send, self.sems[6], at_feat(half, 1 + 2 * k, 0))
                    if self.kind == 1:
                        self.send_back(half, 3 + 2 * k, 0, 4)

        def arrived(self):
            wait(self.sems[6], self.full.at[pl.ds(0, 8)])
            if self.kind == 1:
                for half in range(2):
                    self.send_back(half, 2, 0, 4)

        def swap(self):
            self.arrived()
            send(
                self.full.at[:, :, pl.ds(rows, rows // 2)],
                self.cross,
                net.cross_sends[self.v],
                self.sems[3],
                sibling,
            )

        def apply(self):
            if self.kind == 0:
                wait(self.sems[3], self.cross)
            else:
                self.arrived()
            other = 1 - self.v

            @pl.loop(0, rows // 128)
            def _(step):
                here = pl.ds(pl.multiple_of(step * 128, 128), 128)

                def direct(first, right):
                    width = right.shape[0]
                    left = self.full[pl.ds(step * 8, 8), :, pl.ds(first, width)]
                    return jnp.dot(
                        left.reshape(128, width), right, preferred_element_type=F32
                    )

                def columns(first):
                    return pl.ds(pl.multiple_of(first + step * 128, 128), 128)

                if self.kind == 0:
                    value = direct(0, normed[other, 0])
                    value += direct(rows, normed[other, 1, cross_rows(step // 2, core), :])
                    theirs = lax.rem(step // 2 + 1 - core, 2)
                    first = pl.multiple_of(lax.rem(step, 2) * 128, 128)
                    left = self.cross[pl.ds(theirs * 16, 16), :, pl.ds(first, 128)]
                    value += mirrored(left, normed[other, 1, cross_rows(theirs, 0), :])
                elif self.kind == 1:
                    value = direct(0, normed[other, 2]) + direct(rows, normed[other, 7])
                else:
                    value = direct(0, normed[other, 4 + turned])
                    left = self.full[:, :, columns(512)]
                    value += mirrored(left, normed[other, 5 - turned])
                add(other, here, value)

            begun.add(other)

        def apply_back(self):
            wait(self.sems[3], self.back)
            other = 1 - self.v

            @pl.loop(0, rows // 128)
            def _(step):
                here = pl.ds(pl.multiple_of(step * 128, 128), 128)
                value = mirrored(self.back[0, :, :, here], normed[other, 6])
                value += mirrored(self.back[1, :, :, here], normed[other, 3])
                add(other, here, value)

            begun.add(other)

        def stages(self):
            reduce = [self.product, self.pass_on, self.turn, self.reduced]
            if self.kind == 0:
                return reduce + [self.gather, self.gather_on, self.swap, self.apply]
            if self.kind == 1:
                return reduce + [self.gather, self.gather_on, self.apply, self.apply_back]
            return reduce + [self.spread, self.gather, self.gather_on, self.apply]

    same_items = []
    extras = []

    def diagonal():
        def step_sum(step, carry):
            here = pl.ds(pl.multiple_of(step * 64, 64), 64)
            both = normed[0, 0, here, :].astype(F32) * normed[1, 0, here, :].astype(F32)
            return carry + jnp.sum(both.reshape(8, 8, -1), axis=0)

        part = lax.fori_loop(0, rows // 64, step_sum, zero)
        same[batch] = part
        same_items.append(exchange(same))

    def unit_of(v, here):
        values = views[v][here, :].astype(F32)
        return (values - moments[pl.ds(2 * v, 1), :]) * moments[pl.ds(2 * v + 1, 1), :]

    def back_sums(v, last):
        def step_sum(step, carry):
            here = pl.ds(pl.multiple_of(step * 64, 64), 64)
            back = (2.0 * LAMBDA / total) * acc[v, here, :]
            back += extras[0] * normed[1 - v, 0, here, :].astype(F32)
            acc[v, here, :] = back
            first = carry[0] + jnp.sum(back.reshape(8, 8, -1), axis=0)
            second = carry[1] + jnp.sum((back * unit_of(v, here)).reshape(8, 8, -1), axis=0)
            return first, second

        first, second = lax.fori_loop(0, rows // 64, step_sum, (zero, zero))
        last[batch, pl.ds(0, 1), :] = jnp.sum(first, axis=0, keepdims=True)
        last[batch, pl.ds(1, 1), :] = jnp.sum(second, axis=0, keepdims=True)
        last[batch, pl.ds(2, 6), :] = jnp.zeros((6, rows), F32)
        return exchange(last)

    def finish(v, last, items, out):
        both = collect(last, items) / total
        first, second = both[0:1], both[1:2]

        @pl.loop(0, rows // 64)
        def _(step):
            here = pl.ds(pl.multiple_of(step * 64, 64), 64)
            scale = moments[pl.ds(2 * v + 1, 1), :]
            value = scale * (acc[v, here, :] - first - unit_of(v, here) * second)
            out[here, :] = value.astype(BF16)

    plan = []

    def add_rows(name, ticks):
        plan.extend(zip(ticks, name))

    add_rows([lambda v=v: own_rows(v) for v in (1, 0)], ROWS[0])
    add_rows([diagonal], ROWS[1])
    for n, v in enumerate((1, 0)):
        steps = [lambda v=v, f=f: f(v) for f in (near_rows, take_near, far_rows, take_far)]
        add_rows(steps, ROWS[2 + n])
    for v, kind, ticks in BLOCKS:
        add_rows(Block(v, kind).stages(), ticks)
    def early():
        cosine = jnp.sum(collect(same, same_items[0]), axis=0, keepdims=True) / total
        extra = (2.0 * (cosine - 1.0)).astype(BF16).astype(F32) - 2.0 * LAMBDA * cosine
        extras.append(extra)
        extras.append(back_sums(0, last_a))

    add_rows([early], (max(ticks[-1] for v, _, ticks in BLOCKS if v == 1),))
    for _, step in sorted(plan, key=lambda item: item[0]):
        step()
    items_b = back_sums(1, last_b)
    finish(0, last_a, extras[1], ga)
    finish(1, last_b, items_b, gb)
    net.finish()
    assert (len(net.sends), net.receives) == (SENDS, RECEIVES)


def body(view_a, view_b):
    rows, width = view_a.shape
    total = rows * lax.axis_size("batch")
    blocks = []
    for _ in range(2):
        for columns, wide in zip(REDUCED, GATHERED):
            blocks += [
                pltpu.VMEM((32, 16, columns), BF16),
                pltpu.VMEM((2, 2, 2, 16, columns), BF16),
                pltpu.VMEM((2, 2, 4, 16, columns), BF16),
                pltpu.VMEM((2, 3, 16, columns), BF16),
                pltpu.VMEM((32, 16, wide), BF16),
            ]
    vmem = pl.BlockSpec(memory_space=pltpu.VMEM)
    return pl.pallas_call(
        functools.partial(kernel, rows, total),
        out_shape=(jax.ShapeDtypeStruct((rows, width), BF16),) * 2,
        in_specs=[vmem, vmem],
        out_specs=(vmem, vmem),
        scratch_shapes=[
            pltpu.VMEM((2, 8, rows, width), BF16),
            pltpu.VMEM((2, 8, rows, width), BF16),
            pltpu.VMEM((8, 8, width), F32),
            pltpu.VMEM((8, 8, width), F32),
            pltpu.VMEM((8, 8, width), F32),
            pltpu.VMEM((8, 8, width), F32),
            pltpu.VMEM((8, width), F32),
            pltpu.VMEM((2, rows, width), F32),
            pltpu.VMEM((2, 32, 16, 256), BF16),
            pltpu.VMEM((2, 2, 32, 16, 512), BF16),
            pltpu.SemaphoreType.DMA((SENDS,)),
            pltpu.SemaphoreType.DMA((RECEIVES,)),
        ]
        + blocks,
        compiler_params=pltpu.CompilerParams(
            collective_id=0, has_side_effects=True, vmem_limit_bytes=56 * 2**20
        ),
        name="gram_gradient",
    )(view_a, view_b)


def solution(mesh):
    return jax.shard_map(
        body,
        mesh=mesh,
        in_specs=(P("batch", "feat"), P("batch", "feat")),
        out_specs=(P("batch", "feat"), P("batch", "feat")),
        check_vma=False,
    )
```

```python
import functools

import jax
import jax.numpy as jnp
from jax import lax
from jax.experimental import pallas as pl
from jax.experimental.pallas import tpu as pltpu
from jax.sharding import PartitionSpec as P

LAMBDA = 0.0051
MESH = pl.DeviceIdType.MESH
F32 = jnp.float32
BF16 = jnp.bfloat16
SENDS, RECEIVES = 22, 60
REDUCED = (640, 1024, 512)
GATHERED = (640, 1024, 1024)
ROWS = ((0, 1), (2,), (7, 8, 14, 22, 26), (16, 20, 17, 30, 32))
BLOCKS = (
    (1, 0, (5, 6, 11, 15, 41, 46, 49, 56)),
    (0, 0, (3, 4, 9, 12, 19, 23, 27, 36)),
    (1, 1, (10, 13, 18, 24, 29, 35, 40, 52)),
    (1, 2, (28, 34, 38, 43, 47, 51, 55, 59)),
    (0, 1, (21, 25, 31, 39, 44, 48, 53, 58)),
    (0, 2, (33, 37, 42, 45, 50, 54, 57, 60)),
)


def rem4(value):
    return lax.rem(value, 4)


class Net:
    def __init__(self, send_sems, recv_sems):
        self.send_sems, self.recv_sems = send_sems, recv_sems
        self.sends, self.receives = [], 0

    def sender(self, moved):
        self.sends.append(moved)
        return self.send_sems.at[len(self.sends) - 1]

    def receiver(self):
        self.receives += 1
        return self.recv_sems.at[self.receives - 1]

    def finish(self):
        for n, moved in enumerate(self.sends):
            wait(self.send_sems.at[n], moved)


def send(src, dst, sender, receiver, device):
    pltpu.make_async_remote_copy(
        src_ref=src,
        dst_ref=dst,
        send_sem=sender,
        recv_sem=receiver,
        device_id=device,
        device_id_type=MESH,
    ).start()


def wait(sem, moved):
    pltpu.make_async_copy(moved, moved, sem).wait()


def kernel(rows, total, va, vb, ga, gb, *scratch):
    (raw, normed, stat, same, last_a, last_b, moments, acc, cross, back, send_sems, recv_sems) = scratch[:12]
    blocks = scratch[12:]
    net = Net(send_sems, recv_sems)
    views = (va, vb)
    batch, feat = lax.axis_index("batch"), lax.axis_index("feat")
    x, core = batch // 2, lax.rem(batch, 2)
    y, z = feat // 4, rem4(feat)

    def at_batch(dx, dcore):
        return (rem4(x + dx) * 2 + lax.rem(core + dcore, 2), feat)

    def at_feat(half, d1, d2):
        dy, dz = (d1, d2) if half == 0 else (d2, d1)
        return (batch, rem4(y + dy) * 4 + rem4(z + dz))

    peers = [(lax.rem(batch + k, 8), feat) for k in (4, 3, 5, 2, 6, 1, 7)]
    planes = [at_feat(half, k, 0) for half in range(2) for k in range(1, 4)]
    barrier = pltpu.get_barrier_semaphore()
    for device in peers + planes:
        pl.semaphore_signal(barrier, inc=1, device_id=device, device_id_type=MESH)

    def sums(step, carry):
        out = []
        for v in range(2):
            values = views[v][pl.ds(pl.multiple_of(step * 64, 64), 64), :].astype(F32)
            out.append(carry[2 * v] + jnp.sum(values.reshape(8, 8, -1), axis=0))
            out.append(carry[2 * v + 1] + jnp.sum((values * values).reshape(8, 8, -1), axis=0))
        return tuple(out)

    zero = jnp.zeros((8, rows), F32)
    parts = lax.fori_loop(0, rows // 64, sums, (zero,) * 4)
    for k in range(4):
        stat[batch, pl.ds(k, 1), :] = jnp.sum(parts[k], axis=0, keepdims=True)
    stat[batch, pl.ds(4, 4), :] = jnp.zeros((4, rows), F32)

    pl.semaphore_wait(barrier, len(peers) + len(planes))

    def exchange(ref, count=8):
        used = pl.ds(0, count)
        sender, receiver = net.sender(ref.at[pl.ds(0, 7), used]), net.receiver()
        for device in peers:
            send(ref.at[batch, used], ref.at[batch, used], sender, receiver, device)
        return receiver

    def collect(ref, receiver, count=8):
        wait(receiver, ref.at[pl.ds(0, 7), pl.ds(0, count)])
        result = ref[0]
        for k in range(1, 8):
            result = result + ref[k]
        return result

    stat_items = exchange(stat, 4)
    sibling = (batch + 1 - 2 * core, feat)
    half = rows // 2
    upper, lower = pl.ds(0, half), pl.ds(half, half)
    view_sends = [net.sender(raw.at[v, pl.ds(0, 7)]) for v in range(2)]
    view_sems = [[net.receiver() for _ in range(7)] for _ in range(2)]

    def send_rows(v, src, slot, device, part=None):
        dst = raw.at[v, slot] if part is None else raw.at[v, slot, part]
        send(src, dst, view_sends[v], view_sems[v][slot - 1], device)

    def wait_rows(v, slot):
        wait(view_sems[v][slot - 1], raw.at[v, slot])

    def send_near(v):
        send_rows(v, views[v], 6, at_batch(1, 0))
        send_rows(v, views[v], 2, at_batch(3, 0))

    send_near(1)
    for v in (1, 0):
        send_rows(v, views[v], 1, sibling)

    sum_all = collect(stat, stat_items, 4)
    for v in range(2):
        mean = sum_all[2 * v : 2 * v + 1] / total
        square = sum_all[2 * v + 1 : 2 * v + 2] / total
        moments[pl.ds(2 * v, 1), :] = mean
        moments[pl.ds(2 * v + 1, 1), :] = lax.rsqrt(square - mean * mean + 1e-05)

    def normalize(v, slot):
        source = views[v] if slot == 0 else raw.at[v, slot]

        @pl.loop(0, rows // 64)
        def _(step):
            here = pl.ds(pl.multiple_of(step * 64, 64), 64)
            values = source[here, :].astype(F32)
            unit = (values - moments[pl.ds(2 * v, 1), :]) * moments[pl.ds(2 * v + 1, 1), :]
            normed[v, slot, here, :] = unit.astype(BF16)

    def own_rows(v):
        normalize(v, 0)
        wait_rows(v, 1)
        normalize(v, 1)

    def near_rows(v):
        wait_rows(v, 6)
        wait_rows(v, 2)
        send_rows(v, raw.at[v, 2], 3, sibling)
        send_rows(v, raw.at[v, 6], 7, sibling)
        if v == 1:
            send_near(0)

    def take_near(v):
        normalize(v, 2)
        normalize(v, 6)
        for slot in (3, 7):
            wait_rows(v, slot)
            normalize(v, slot)

    def pass_far(v):
        send_rows(v, raw.at[v, 6, upper], 4, at_batch(1, 0), upper)
        send_rows(v, raw.at[v, 2, lower], 4, at_batch(3, 0), lower)

    def far_rows(v):
        wait_rows(v, 4)
        send_rows(v, raw.at[v, 4], 5, sibling)

    def take_far(v):
        normalize(v, 4)
        wait_rows(v, 5)
        normalize(v, 5)

    net.cross_sends = [net.sender(cross.at[v]) for v in range(2)]
    net.back_sends = [net.sender(back.at[v]) for v in range(2)]
    begun = set()

    def cross_rows(part, turn):
        return pl.ds(pl.multiple_of(lax.rem(part + turn, 2) * 256, 256), 256)

    def tile(step):
        return pl.ds(pl.multiple_of(step * 128, 128), 128)

    def partner(step):
        return rem4(step + 2 + (step // 2) * (1 + 2 * lax.rem(step, 2)))

    turned = x // 2

    def mirrored(left, right):
        return lax.dot_general(
            left.reshape(-1, 128), right, (((0,), (0,)), ((), ())), preferred_element_type=F32
        )

    def add(v, here, value):
        acc[v, here, :] = acc[v, here, :] + value if v in begun else value

    class Block:
        def __init__(self, v, kind):
            self.v, self.kind = v, kind
            base = (v * 3 + kind) * 5
            self.part, self.r1, self.r2, self.r3, self.full = blocks[base : base + 5]
            self.cross, self.back = cross.at[v], back.at[v]
            self.columns = REDUCED[kind]
            mirrored = 1 if kind == 2 else 0
            self.reduce_send = net.sender(self.part.at[pl.ds(0, 30)])
            self.gather_send = net.sender(self.full.at[pl.ds(0, 30 + mirrored)])
            self.sems = [net.receiver() for _ in range(7)]

        def mine(self, half):
            return (y, z) if half == 0 else (z, y)

        def product(self):
            v = self.v
            @pl.loop(0, rows // 128)
            def _(step):
                left = normed[v, 0, pl.ds(pl.multiple_of(step * 128, 128), 128), :]

                def block(first, right):
                    value = lax.dot_general(
                        left, right, (((1,), (1,)), ((), ())), preferred_element_type=F32
                    )
                    width = right.shape[0]
                    self.part[pl.ds(step * 8, 8), :, pl.ds(first, width)] = value.astype(
                        BF16
                    ).reshape(8, 16, width)

                if self.kind == 0:
                    block(0, normed[v, 0, cross_rows(step // 2, 0), :])
                    block(256, normed[v, 0, tile(partner(step)), :])
                    block(384, normed[v, 1, cross_rows(step // 2, core), :])
                elif self.kind == 1:
                    block(0, normed[v, 2])
                    block(rows, normed[v, 7])
                else:
                    block(0, normed[v, 4 + turned])

            for half in range(2):
                m1, _ = self.mine(half)
                base = half * 16 + rem4(m1 + 2) * 4
                for k in range(2):
                    send(
                        self.part.at[pl.ds(base + 2 * (1 - k), 2)],
                        self.r1.at[half, k],
                        self.reduce_send,
                        self.sems[0],
                        at_feat(half, 1 + 2 * k, 0),
                    )

        def pass_on(self):
            wait(self.sems[0], self.r1)
            for half in range(2):
                m1, _ = self.mine(half)
                for k in range(2):
                    base = half * 16 + rem4(m1 + 1 + 2 * k) * 4
                    here = pl.ds(base + 2 * (1 - k), 2)
                    self.part[here] = (
                        self.part[here].astype(F32) + self.r1[half, k].astype(F32)
                    ).astype(BF16)
                    send(
                        self.part.at[pl.ds(base, 4)],
                        self.r2.at[half, k],
                        self.reduce_send,
                        self.sems[1],
                        at_feat(half, 1 + 2 * k, 0),
                    )

        def turn(self):
            wait(self.sems[1], self.r2)
            for half in range(2):
                m1, m2 = self.mine(half)
                base = half * 16 + m1 * 4
                here = pl.ds(base, 4)
                self.part[here] = (
                    self.part[here].astype(F32)
                    + self.r2[half, 0].astype(F32)
                    + self.r2[half, 1].astype(F32)
                ).astype(BF16)
                for k in range(1, 4):
                    send(
                        self.part.at[base + rem4(m2 + k)],
                        self.r3.at[half, k - 1],
                        self.reduce_send,
                        self.sems[2],
                        at_feat(half, 0, k),
                    )

        def own(self, half):
            m1, m2 = self.mine(half)
            return half * 16 + m1 * 4 + m2

        def mirror(self, own, first, start, device):
            send(
                self.full.at[own, :, pl.ds(first, 512)],
                self.full.at[own, :, pl.ds(start, 512)],
                self.gather_send,
                self.sems[3],
                device,
            )

        def reduced(self):
            wait(self.sems[2], self.r3)
            for half in range(2):
                own = self.own(half)
                value = self.part[own].astype(F32)
                for k in range(3):
                    value = value + self.r3[half, k].astype(F32)
                self.full[own, :, pl.ds(0, self.columns)] = value.astype(BF16)
                if self.kind == 2:
                    self.mirror(own, 0, 512, at_batch(2, turned))
            if self.kind != 2:
                self.spread()

        def spread(self):
            if self.kind == 2:
                wait(self.sems[3], self.full.at[pl.ds(0, 1)])
            for half in range(2):
                here = self.full.at[self.own(half)]
                for k in range(1, 4):
                    send(here, here, self.gather_send, self.sems[4], at_feat(half, 0, k))

        def send_back(self, half, ahead, first, count):
            m1, _ = self.mine(half)
            chunks = pl.ds(half * 16 + rem4(m1 + ahead) * 4 + first, count)
            for k, device in enumerate((at_batch(1, 0), at_batch(3, 1))):
                send(
                    self.full.at[chunks, :, pl.ds(512 * k, 512)],
                    self.back.at[k, chunks],
                    net.back_sends[self.v],
                    self.sems[3],
                    device,
                )

        def gather(self):
            wait(self.sems[4], self.full.at[pl.ds(0, 6)])
            for half in range(2):
                m1, _ = self.mine(half)
                here = self.full.at[pl.ds(half * 16 + m1 * 4, 4)]
                for k in range(2):
                    send(here, here, self.gather_send, self.sems[5], at_feat(half, 1 + 2 * k, 0))
                if self.kind == 1:
                    self.send_back(half, 0, 0, 4)

        def gather_on(self):
            wait(self.sems[5], self.full.at[pl.ds(0, 16)])
            for half in range(2):
                m1, _ = self.mine(half)
                for k in range(2):
                    base = half * 16 + rem4(m1 + 3 + 2 * k) * 4
                    here = self.full.at[pl.ds(base + 2 * k, 2)]
                    send(here, here, self.gather_send, self.sems[6], at_feat(half, 1 + 2 * k, 0))
                    if self.kind == 1:
                        self.send_back(half, 3 + 2 * k, 0, 4)

        def arrived(self):
            wait(self.sems[6], self.full.at[pl.ds(0, 8)])
            if self.kind == 1:
                for half in range(2):
                    self.send_back(half, 2, 0, 4)

        def swap(self):
            self.arrived()
            send(
                self.full.at[:, :, pl.ds(384, 256)],
                self.cross,
                net.cross_sends[self.v],
                self.sems[3],
                sibling,
            )

        def apply(self):
            if self.kind == 0:
                wait(self.sems[3], self.cross)
            else:
                self.arrived()
            other = 1 - self.v

            @pl.loop(0, rows // 128)
            def _(step):
                here = pl.ds(pl.multiple_of(step * 128, 128), 128)

                def direct(first, right):
                    width = right.shape[0]
                    left = self.full[pl.ds(step * 8, 8), :, pl.ds(first, width)]
                    return jnp.dot(
                        left.reshape(128, width), right, preferred_element_type=F32
                    )

                def columns(first):
                    return pl.ds(pl.multiple_of(first + step * 128, 128), 128)

                if self.kind == 0:
                    value = direct(0, normed[other, 0, cross_rows(step // 2, 0), :])
                    value += direct(256, normed[other, 0, tile(partner(step)), :])
                    value += direct(384, normed[other, 1, cross_rows(step // 2, core), :])
                    taker = 3 - step + (step // 2) * (2 * step - 5)
                    left = self.full[pl.ds(taker * 8, 8), :, pl.ds(256, 128)]
                    value += mirrored(left, normed[other, 0, tile(taker), :])
                    theirs = lax.rem(step // 2 + 1 - core, 2)
                    first = pl.multiple_of(lax.rem(step, 2) * 128, 128)
                    left = self.cross[pl.ds(theirs * 16, 16), :, pl.ds(first, 128)]
                    value += mirrored(left, normed[other, 1, cross_rows(theirs, 0), :])
                elif self.kind == 1:
                    value = direct(0, normed[other, 2]) + direct(rows, normed[other, 7])
                else:
                    value = direct(0, normed[other, 4 + turned])
                    left = self.full[:, :, columns(512)]
                    value += mirrored(left, normed[other, 5 - turned])
                add(other, here, value)

            begun.add(other)

        def apply_back(self):
            wait(self.sems[3], self.back)
            other = 1 - self.v

            @pl.loop(0, rows // 128)
            def _(step):
                here = pl.ds(pl.multiple_of(step * 128, 128), 128)
                value = mirrored(self.back[0, :, :, here], normed[other, 6])
                value += mirrored(self.back[1, :, :, here], normed[other, 3])
                add(other, here, value)

            begun.add(other)

        def stages(self):
            reduce = [self.product, self.pass_on, self.turn, self.reduced]
            if self.kind == 0:
                return reduce + [self.gather, self.gather_on, self.swap, self.apply]
            if self.kind == 1:
                return reduce + [self.gather, self.gather_on, self.apply, self.apply_back]
            return reduce + [self.spread, self.gather, self.gather_on, self.apply]

    same_items = []
    extras = []

    def diagonal():
        def step_sum(step, carry):
            here = pl.ds(pl.multiple_of(step * 64, 64), 64)
            both = normed[0, 0, here, :].astype(F32) * normed[1, 0, here, :].astype(F32)
            return carry + jnp.sum(both.reshape(8, 8, -1), axis=0)

        part = lax.fori_loop(0, rows // 64, step_sum, zero)
        same[batch] = part
        same_items.append(exchange(same))

    def unit_of(v, here):
        values = views[v][here, :].astype(F32)
        return (values - moments[pl.ds(2 * v, 1), :]) * moments[pl.ds(2 * v + 1, 1), :]

    def back_sums(v, last):
        def step_sum(step, carry):
            here = pl.ds(pl.multiple_of(step * 64, 64), 64)
            back = (2.0 * LAMBDA / total) * acc[v, here, :]
            back += extras[0] * normed[1 - v, 0, here, :].astype(F32)
            acc[v, here, :] = back
            first = carry[0] + jnp.sum(back.reshape(8, 8, -1), axis=0)
            second = carry[1] + jnp.sum((back * unit_of(v, here)).reshape(8, 8, -1), axis=0)
            return first, second

        first, second = lax.fori_loop(0, rows // 64, step_sum, (zero, zero))
        last[batch, pl.ds(0, 1), :] = jnp.sum(first, axis=0, keepdims=True)
        last[batch, pl.ds(1, 1), :] = jnp.sum(second, axis=0, keepdims=True)
        last[batch, pl.ds(2, 6), :] = jnp.zeros((6, rows), F32)
        return exchange(last, 2)

    def finish(v, last, items, out):
        both = collect(last, items, 2) / total
        first, second = both[0:1], both[1:2]

        @pl.loop(0, rows // 64)
        def _(step):
            here = pl.ds(pl.multiple_of(step * 64, 64), 64)
            scale = moments[pl.ds(2 * v + 1, 1), :]
            value = scale * (acc[v, here, :] - first - unit_of(v, here) * second)
            out[here, :] = value.astype(BF16)

    plan = []

    def add_rows(name, ticks):
        plan.extend(zip(ticks, name))

    add_rows([lambda v=v: own_rows(v) for v in (1, 0)], ROWS[0])
    add_rows([diagonal], ROWS[1])
    for n, v in enumerate((1, 0)):
        steps = [lambda v=v, f=f: f(v) for f in (near_rows, take_near, pass_far, far_rows, take_far)]
        add_rows(steps, ROWS[2 + n])
    for v, kind, ticks in BLOCKS:
        add_rows(Block(v, kind).stages(), ticks)
    def early():
        cosine = jnp.sum(collect(same, same_items[0]), axis=0, keepdims=True) / total
        extra = (2.0 * (cosine - 1.0)).astype(BF16).astype(F32) - 2.0 * LAMBDA * cosine
        extras.append(extra)
        extras.append(back_sums(0, last_a))

    add_rows([early], (max(ticks[-1] for v, _, ticks in BLOCKS if v == 1),))
    for _, step in sorted(plan, key=lambda item: item[0]):
        step()
    items_b = back_sums(1, last_b)
    finish(0, last_a, extras[1], ga)
    finish(1, last_b, items_b, gb)
    net.finish()
    assert (len(net.sends), net.receives) == (SENDS, RECEIVES)


def body(view_a, view_b):
    rows, width = view_a.shape
    total = rows * lax.axis_size("batch")
    blocks = []
    for _ in range(2):
        for columns, wide in zip(REDUCED, GATHERED):
            blocks += [
                pltpu.VMEM((32, 16, columns), BF16),
                pltpu.VMEM((2, 2, 2, 16, columns), BF16),
                pltpu.VMEM((2, 2, 4, 16, columns), BF16),
                pltpu.VMEM((2, 3, 16, columns), BF16),
                pltpu.VMEM((32, 16, wide), BF16),
            ]
    vmem = pl.BlockSpec(memory_space=pltpu.VMEM)
    return pl.pallas_call(
        functools.partial(kernel, rows, total),
        out_shape=(pltpu.VMEM((rows, width), BF16),) * 2,
        in_specs=[vmem, vmem],
        out_specs=(vmem, vmem),
        scratch_shapes=[
            pltpu.VMEM((2, 8, rows, width), BF16),
            pltpu.VMEM((2, 8, rows, width), BF16),
            pltpu.VMEM((8, 8, width), F32),
            pltpu.VMEM((8, 8, width), F32),
            pltpu.VMEM((8, 8, width), F32),
            pltpu.VMEM((8, 8, width), F32),
            pltpu.VMEM((8, width), F32),
            pltpu.VMEM((2, rows, width), F32),
            pltpu.VMEM((2, 32, 16, 256), BF16),
            pltpu.VMEM((2, 2, 32, 16, 512), BF16),
            pltpu.SemaphoreType.DMA((SENDS,)),
            pltpu.SemaphoreType.DMA((RECEIVES,)),
        ]
        + blocks,
        compiler_params=pltpu.CompilerParams(
            collective_id=0, has_side_effects=True, vmem_limit_bytes=56 * 2**20
        ),
        name="gram_gradient",
    )(view_a, view_b)


def solution(mesh):
    return jax.shard_map(
        body,
        mesh=mesh,
        in_specs=(P("batch", "feat"), P("batch", "feat")),
        out_specs=(P("batch", "feat"), P("batch", "feat")),
        check_vma=False,
    )
```

```python
import functools

import jax
import jax.numpy as jnp
from jax import lax
from jax.experimental import pallas as pl
from jax.experimental.pallas import tpu as pltpu
from jax.sharding import PartitionSpec as P

LAMBDA = 0.0051
MESH = pl.DeviceIdType.MESH
F32 = jnp.float32
BF16 = jnp.bfloat16
SENDS, RECEIVES = 22, 60
REDUCED = (640, 1024, 512)
GATHERED = (640, 1024, 1024)
ROWS = ((0, 1), (20,), (5, 6, 8, 23, 27), (13, 17, 14, 26, 30))
BLOCKS = (
    (1, 0, (2, 3, 7, 11, 16, 21, 36, 40)),
    (0, 0, (4, 10, 15, 22, 39, 45, 51, 56)),
    (1, 1, (9, 12, 18, 24, 28, 33, 41, 54)),
    (1, 2, (29, 34, 38, 43, 47, 50, 55, 59)),
    (0, 1, (19, 25, 31, 37, 44, 48, 53, 58)),
    (0, 2, (32, 35, 42, 46, 49, 52, 57, 60)),
)


def rem4(value):
    return lax.rem(value, 4)


class Net:
    def __init__(self, send_sems, recv_sems):
        self.send_sems, self.recv_sems = send_sems, recv_sems
        self.sends, self.receives = [], 0

    def sender(self, moved):
        self.sends.append(moved)
        return self.send_sems.at[len(self.sends) - 1]

    def receiver(self):
        self.receives += 1
        return self.recv_sems.at[self.receives - 1]

    def finish(self):
        for n, moved in enumerate(self.sends):
            wait(self.send_sems.at[n], moved)


def send(src, dst, sender, receiver, device):
    pltpu.make_async_remote_copy(
        src_ref=src,
        dst_ref=dst,
        send_sem=sender,
        recv_sem=receiver,
        device_id=device,
        device_id_type=MESH,
    ).start()


def wait(sem, moved):
    pltpu.make_async_copy(moved, moved, sem).wait()


def kernel(rows, total, far_a, far_b, ga, gb, moments, *scratch):
    (raw, normed, stat, same, last_a, last_b, acc, cross, back, own, own_sems, send_sems, recv_sems) = scratch[:13]
    blocks = scratch[13:]
    net = Net(send_sems, recv_sems)
    views = (own.at[0], own.at[1])
    loads = [
        pltpu.make_async_copy(source, own.at[v], own_sems.at[v])
        for v, source in enumerate((far_a, far_b))
    ]
    for load in loads:
        load.start()
    batch, feat = lax.axis_index("batch"), lax.axis_index("feat")
    x, core = batch // 2, lax.rem(batch, 2)
    y, z = feat // 4, rem4(feat)

    def at_batch(dx, dcore):
        return (rem4(x + dx) * 2 + lax.rem(core + dcore, 2), feat)

    def at_feat(half, d1, d2):
        dy, dz = (d1, d2) if half == 0 else (d2, d1)
        return (batch, rem4(y + dy) * 4 + rem4(z + dz))

    peers = [(lax.rem(batch + k, 8), feat) for k in (4, 3, 5, 2, 6, 1, 7)]
    planes = [at_feat(half, k, 0) for half in range(2) for k in range(1, 4)]
    barrier = pltpu.get_barrier_semaphore()
    for device in peers + planes:
        pl.semaphore_signal(barrier, inc=1, device_id=device, device_id_type=MESH)

    def sums(step, carry):
        out = []
        for v in range(2):
            values = views[v][pl.ds(pl.multiple_of(step * 64, 64), 64), :].astype(F32)
            out.append(carry[2 * v] + jnp.sum(values.reshape(8, 8, -1), axis=0))
            out.append(carry[2 * v + 1] + jnp.sum((values * values).reshape(8, 8, -1), axis=0))
        return tuple(out)

    zero = jnp.zeros((8, rows), F32)
    for load in loads:
        load.wait()
    parts = lax.fori_loop(0, rows // 64, sums, (zero,) * 4)
    for k in range(4):
        stat[batch, pl.ds(k, 1), :] = jnp.sum(parts[k], axis=0, keepdims=True)
    stat[batch, pl.ds(4, 4), :] = jnp.zeros((4, rows), F32)

    pl.semaphore_wait(barrier, len(peers) + len(planes))

    def exchange(ref, count=8):
        used = pl.ds(0, count)
        sender, receiver = net.sender(ref.at[pl.ds(0, 7), used]), net.receiver()
        for device in peers:
            send(ref.at[batch, used], ref.at[batch, used], sender, receiver, device)
        return receiver

    def collect(ref, receiver, count=8):
        wait(receiver, ref.at[pl.ds(0, 7), pl.ds(0, count)])
        result = ref[0]
        for k in range(1, 8):
            result = result + ref[k]
        return result

    stat_items = exchange(stat, 4)
    sibling = (batch + 1 - 2 * core, feat)
    half = rows // 2
    upper, lower = pl.ds(0, half), pl.ds(half, half)
    view_sends = [net.sender(raw.at[v, pl.ds(0, 7)]) for v in range(2)]
    view_sems = [[net.receiver() for _ in range(7)] for _ in range(2)]

    def send_rows(v, src, slot, device, part=None):
        dst = raw.at[v, slot] if part is None else raw.at[v, slot, part]
        send(src, dst, view_sends[v], view_sems[v][slot - 1], device)

    def wait_rows(v, slot):
        wait(view_sems[v][slot - 1], raw.at[v, slot])

    def send_near(v):
        send_rows(v, views[v], 6, at_batch(1, 0))
        send_rows(v, views[v], 2, at_batch(3, 0))

    send_near(1)
    for v in (1, 0):
        send_rows(v, views[v], 1, sibling)
    send_near(0)

    sum_all = collect(stat, stat_items, 4)
    for v in range(2):
        mean = sum_all[2 * v : 2 * v + 1] / total
        square = sum_all[2 * v + 1 : 2 * v + 2] / total
        moments[pl.ds(2 * v, 1), :] = mean
        moments[pl.ds(2 * v + 1, 1), :] = lax.rsqrt(square - mean * mean + 1e-05)

    def normalize(v, slot):
        source = views[v] if slot == 0 else raw.at[v, slot]

        @pl.loop(0, rows // 64)
        def _(step):
            here = pl.ds(pl.multiple_of(step * 64, 64), 64)
            values = source[here, :].astype(F32)
            unit = (values - moments[pl.ds(2 * v, 1), :]) * moments[pl.ds(2 * v + 1, 1), :]
            normed[v, slot, here, :] = unit.astype(BF16)

    def own_rows(v):
        normalize(v, 0)
        wait_rows(v, 1)
        normalize(v, 1)

    def near_rows(v):
        wait_rows(v, 6)
        wait_rows(v, 2)
        send_rows(v, raw.at[v, 2], 3, sibling)
        send_rows(v, raw.at[v, 6], 7, sibling)

    def take_near(v):
        normalize(v, 2)
        normalize(v, 6)
        for slot in (3, 7):
            wait_rows(v, slot)
            normalize(v, slot)

    def pass_far(v):
        send_rows(v, raw.at[v, 6, upper], 4, at_batch(1, 0), upper)
        send_rows(v, raw.at[v, 2, lower], 4, at_batch(3, 0), lower)

    def far_rows(v):
        wait_rows(v, 4)
        send_rows(v, raw.at[v, 4], 5, sibling)

    def take_far(v):
        normalize(v, 4)
        wait_rows(v, 5)
        normalize(v, 5)

    net.cross_sends = [net.sender(cross.at[v]) for v in range(2)]
    net.back_sends = [net.sender(back.at[v]) for v in range(2)]
    begun = set()

    def cross_rows(part, turn):
        return pl.ds(pl.multiple_of(lax.rem(part + turn, 2) * 256, 256), 256)

    def tile(step):
        return pl.ds(pl.multiple_of(step * 128, 128), 128)

    def partner(step):
        return rem4(step + 2 + (step // 2) * (1 + 2 * lax.rem(step, 2)))

    turned = x // 2

    def mirrored(left, right):
        return lax.dot_general(
            left.reshape(-1, left.shape[-1]), right, (((0,), (0,)), ((), ())), preferred_element_type=F32
        )

    def add(v, here, value):
        acc[v, here, :] = acc[v, here, :] + value if v in begun else value

    class Block:
        def __init__(self, v, kind):
            self.v, self.kind = v, kind
            base = (v * 3 + kind) * 5
            self.part, self.r1, self.r2, self.r3, self.full = blocks[base : base + 5]
            self.cross, self.back = cross.at[v], back.at[v]
            self.columns = REDUCED[kind]
            mirrored = 1 if kind == 2 else 0
            self.reduce_send = net.sender(self.part.at[pl.ds(0, 30)])
            self.gather_send = net.sender(self.full.at[pl.ds(0, 30 + mirrored)])
            self.sems = [net.receiver() for _ in range(7)]

        def mine(self, half):
            return (y, z) if half == 0 else (z, y)

        def product(self):
            v = self.v
            @pl.loop(0, rows // 128)
            def _(step):
                left = normed[v, 0, pl.ds(pl.multiple_of(step * 128, 128), 128), :]

                def block(first, right):
                    value = lax.dot_general(
                        left, right, (((1,), (1,)), ((), ())), preferred_element_type=F32
                    )
                    width = right.shape[0]
                    self.part[pl.ds(step * 8, 8), :, pl.ds(first, width)] = value.astype(
                        BF16
                    ).reshape(8, 16, width)

                if self.kind == 0:
                    block(0, normed[v, 0, cross_rows(step // 2, 0), :])
                    block(256, normed[v, 0, tile(partner(step)), :])
                    block(384, normed[v, 1, cross_rows(step // 2, core), :])
                elif self.kind == 1:
                    block(0, normed[v, 2])
                    block(rows, normed[v, 7])
                else:
                    block(0, normed[v, 4 + turned])

            for half in range(2):
                m1, _ = self.mine(half)
                base = half * 16 + rem4(m1 + 2) * 4
                for k in range(2):
                    send(
                        self.part.at[pl.ds(base + 2 * (1 - k), 2)],
                        self.r1.at[half, k],
                        self.reduce_send,
                        self.sems[0],
                        at_feat(half, 1 + 2 * k, 0),
                    )

        def pass_on(self):
            wait(self.sems[0], self.r1)
            for half in range(2):
                m1, _ = self.mine(half)
                for k in range(2):
                    base = half * 16 + rem4(m1 + 1 + 2 * k) * 4
                    here = pl.ds(base + 2 * (1 - k), 2)
                    self.part[here] = (
                        self.part[here].astype(F32) + self.r1[half, k].astype(F32)
                    ).astype(BF16)
                    send(
                        self.part.at[pl.ds(base, 4)],
                        self.r2.at[half, k],
                        self.reduce_send,
                        self.sems[1],
                        at_feat(half, 1 + 2 * k, 0),
                    )

        def turn(self):
            wait(self.sems[1], self.r2)
            for half in range(2):
                m1, m2 = self.mine(half)
                base = half * 16 + m1 * 4
                here = pl.ds(base, 4)
                self.part[here] = (
                    self.part[here].astype(F32)
                    + self.r2[half, 0].astype(F32)
                    + self.r2[half, 1].astype(F32)
                ).astype(BF16)
                for k in range(1, 4):
                    send(
                        self.part.at[base + rem4(m2 + k)],
                        self.r3.at[half, k - 1],
                        self.reduce_send,
                        self.sems[2],
                        at_feat(half, 0, k),
                    )

        def own(self, half):
            m1, m2 = self.mine(half)
            return half * 16 + m1 * 4 + m2

        def mirror(self, own, first, start, device):
            send(
                self.full.at[own, :, pl.ds(first, 512)],
                self.full.at[own, :, pl.ds(start, 512)],
                self.gather_send,
                self.sems[3],
                device,
            )

        def reduced(self):
            wait(self.sems[2], self.r3)
            for half in range(2):
                own = self.own(half)
                value = self.part[own].astype(F32)
                for k in range(3):
                    value = value + self.r3[half, k].astype(F32)
                self.full[own, :, pl.ds(0, self.columns)] = value.astype(BF16)
                if self.kind == 2:
                    self.mirror(own, 0, 512, at_batch(2, turned))
            if self.kind != 2:
                self.spread()

        def spread(self):
            if self.kind == 2:
                wait(self.sems[3], self.full.at[pl.ds(0, 1)])
            for half in range(2):
                here = self.full.at[self.own(half)]
                for k in range(1, 4):
                    send(here, here, self.gather_send, self.sems[4], at_feat(half, 0, k))

        def send_back(self, half, ahead, first, count):
            m1, _ = self.mine(half)
            chunks = pl.ds(half * 16 + rem4(m1 + ahead) * 4 + first, count)
            for k, device in enumerate((at_batch(1, 0), at_batch(3, 1))):
                send(
                    self.full.at[chunks, :, pl.ds(512 * k, 512)],
                    self.back.at[k, chunks],
                    net.back_sends[self.v],
                    self.sems[3],
                    device,
                )

        def gather(self):
            wait(self.sems[4], self.full.at[pl.ds(0, 6)])
            for half in range(2):
                m1, _ = self.mine(half)
                here = self.full.at[pl.ds(half * 16 + m1 * 4, 4)]
                for k in range(2):
                    send(here, here, self.gather_send, self.sems[5], at_feat(half, 1 + 2 * k, 0))
                if self.kind == 1:
                    self.send_back(half, 0, 0, 4)

        def gather_on(self):
            wait(self.sems[5], self.full.at[pl.ds(0, 16)])
            for half in range(2):
                m1, _ = self.mine(half)
                for k in range(2):
                    base = half * 16 + rem4(m1 + 3 + 2 * k) * 4
                    here = self.full.at[pl.ds(base + 2 * k, 2)]
                    send(here, here, self.gather_send, self.sems[6], at_feat(half, 1 + 2 * k, 0))
                    if self.kind == 1:
                        self.send_back(half, 3 + 2 * k, 0, 4)

        def arrived(self):
            wait(self.sems[6], self.full.at[pl.ds(0, 8)])
            if self.kind == 1:
                for half in range(2):
                    self.send_back(half, 2, 0, 4)

        def swap(self):
            self.arrived()
            send(
                self.full.at[:, :, pl.ds(384, 256)],
                self.cross,
                net.cross_sends[self.v],
                self.sems[3],
                sibling,
            )

        def apply(self):
            if self.kind == 0:
                wait(self.sems[3], self.cross)
            else:
                self.arrived()
            other = 1 - self.v
            if self.kind == 0:
                self.apply_own(other)
            else:

                @pl.loop(0, 2)
                def _(step):
                    here = pl.ds(pl.multiple_of(step * 256, 256), 256)

                    def direct(first, right):
                        left = self.full[pl.ds(step * 16, 16), :, pl.ds(first, 512)]
                        return jnp.dot(
                            left.reshape(256, 512), right, preferred_element_type=F32
                        )

                    if self.kind == 1:
                        value = direct(0, normed[other, 2]) + direct(rows, normed[other, 7])
                    else:
                        value = direct(0, normed[other, 4 + turned])
                        columns = pl.ds(pl.multiple_of(512 + step * 256, 256), 256)
                        left = self.full[:, :, columns]
                        value += mirrored(left, normed[other, 5 - turned])
                    add(other, here, value)

            begun.add(other)

        def apply_own(self, other):
            @pl.loop(0, rows // 128)
            def _(step):
                here = pl.ds(pl.multiple_of(step * 128, 128), 128)

                def direct(first, right):
                    width = right.shape[0]
                    left = self.full[pl.ds(step * 8, 8), :, pl.ds(first, width)]
                    return jnp.dot(
                        left.reshape(128, width), right, preferred_element_type=F32
                    )

                value = direct(0, normed[other, 0, cross_rows(step // 2, 0), :])
                value += direct(256, normed[other, 0, tile(partner(step)), :])
                value += direct(384, normed[other, 1, cross_rows(step // 2, core), :])
                taker = 3 - step + (step // 2) * (2 * step - 5)
                left = self.full[pl.ds(taker * 8, 8), :, pl.ds(256, 128)]
                value += mirrored(left, normed[other, 0, tile(taker), :])
                theirs = lax.rem(step // 2 + 1 - core, 2)
                first = pl.multiple_of(lax.rem(step, 2) * 128, 128)
                left = self.cross[pl.ds(theirs * 16, 16), :, pl.ds(first, 128)]
                value += mirrored(left, normed[other, 1, cross_rows(theirs, 0), :])
                add(other, here, value)

        def apply_back(self):
            wait(self.sems[3], self.back)
            other = 1 - self.v

            @pl.loop(0, 2)
            def _(step):
                here = pl.ds(pl.multiple_of(step * 256, 256), 256)
                value = mirrored(self.back[0, :, :, here], normed[other, 6])
                value += mirrored(self.back[1, :, :, here], normed[other, 3])
                add(other, here, value)

            begun.add(other)

        def stages(self):
            reduce = [self.product, self.pass_on, self.turn, self.reduced]
            if self.kind == 0:
                return reduce + [self.gather, self.gather_on, self.swap, self.apply]
            if self.kind == 1:
                return reduce + [self.gather, self.gather_on, self.apply, self.apply_back]
            return reduce + [self.spread, self.gather, self.gather_on, self.apply]

    same_items = []
    extras = []

    def diagonal():
        def step_sum(step, carry):
            here = pl.ds(pl.multiple_of(step * 64, 64), 64)
            both = normed[0, 0, here, :].astype(F32) * normed[1, 0, here, :].astype(F32)
            return carry + jnp.sum(both.reshape(8, 8, -1), axis=0)

        part = lax.fori_loop(0, rows // 64, step_sum, zero)
        same[batch] = part
        same_items.append(exchange(same))

    def unit_of(v, here):
        values = views[v][here, :].astype(F32)
        return (values - moments[pl.ds(2 * v, 1), :]) * moments[pl.ds(2 * v + 1, 1), :]

    def back_sums(v, last):
        def step_sum(step, carry):
            here = pl.ds(pl.multiple_of(step * 64, 64), 64)
            back = (2.0 * LAMBDA / total) * acc[v, here, :]
            back += extras[0] * normed[1 - v, 0, here, :].astype(F32)
            acc[v, here, :] = back
            first = carry[0] + jnp.sum(back.reshape(8, 8, -1), axis=0)
            second = carry[1] + jnp.sum((back * unit_of(v, here)).reshape(8, 8, -1), axis=0)
            return first, second

        first, second = lax.fori_loop(0, rows // 64, step_sum, (zero, zero))
        last[batch, pl.ds(0, 1), :] = jnp.sum(first, axis=0, keepdims=True)
        last[batch, pl.ds(1, 1), :] = jnp.sum(second, axis=0, keepdims=True)
        last[batch, pl.ds(2, 6), :] = jnp.zeros((6, rows), F32)
        return exchange(last, 2)

    def finish(v, last, items, out):
        both = collect(last, items, 2) / total
        first, second = both[0:1], both[1:2]

        @pl.loop(0, rows // 64)
        def _(step):
            here = pl.ds(pl.multiple_of(step * 64, 64), 64)
            out[here, :] = acc[v, here, :] - first - unit_of(v, here) * second

    plan = []

    def add_rows(name, ticks):
        plan.extend(zip(ticks, name))

    add_rows([lambda v=v: own_rows(v) for v in (1, 0)], ROWS[0])
    add_rows([diagonal], ROWS[1])
    for n, v in enumerate((1, 0)):
        steps = [lambda v=v, f=f: f(v) for f in (near_rows, take_near, pass_far, far_rows, take_far)]
        add_rows(steps, ROWS[2 + n])
    for v, kind, ticks in BLOCKS:
        add_rows(Block(v, kind).stages(), ticks)
    def early():
        cosine = jnp.sum(collect(same, same_items[0]), axis=0, keepdims=True) / total
        extra = (2.0 * (cosine - 1.0)).astype(BF16).astype(F32) - 2.0 * LAMBDA * cosine
        extras.append(extra)
        extras.append(back_sums(0, last_a))

    add_rows([early], (max(ticks[-1] for v, _, ticks in BLOCKS if v == 1),))
    for _, step in sorted(plan, key=lambda item: item[0]):
        step()
    items_b = back_sums(1, last_b)
    finish(0, last_a, extras[1], ga)
    finish(1, last_b, items_b, gb)
    net.finish()
    assert (len(net.sends), net.receives) == (SENDS, RECEIVES)


def body(view_a, view_b):
    rows, width = view_a.shape
    total = rows * lax.axis_size("batch")
    blocks = []
    for _ in range(2):
        for columns, wide in zip(REDUCED, GATHERED):
            blocks += [
                pltpu.VMEM((32, 16, columns), BF16),
                pltpu.VMEM((2, 2, 2, 16, columns), BF16),
                pltpu.VMEM((2, 2, 4, 16, columns), BF16),
                pltpu.VMEM((2, 3, 16, columns), BF16),
                pltpu.VMEM((32, 16, wide), BF16),
            ]
    vmem = pl.BlockSpec(memory_space=pltpu.VMEM)
    left_a, left_b, moments = pl.pallas_call(
        functools.partial(kernel, rows, total),
        out_shape=(pltpu.VMEM((rows, width), F32),) * 2 + (pltpu.VMEM((8, width), F32),),
        in_specs=[pl.BlockSpec(memory_space=pl.ANY)] * 2,
        out_specs=(vmem, vmem, vmem),
        scratch_shapes=[
            pltpu.VMEM((2, 8, rows, width), BF16),
            pltpu.VMEM((2, 8, rows, width), BF16),
            pltpu.VMEM((8, 8, width), F32),
            pltpu.VMEM((8, 8, width), F32),
            pltpu.VMEM((8, 8, width), F32),
            pltpu.VMEM((8, 8, width), F32),
            pltpu.VMEM((2, rows, width), F32),
            pltpu.VMEM((2, 32, 16, 256), BF16),
            pltpu.VMEM((2, 2, 32, 16, 512), BF16),
            pltpu.VMEM((2, rows, width), BF16),
            pltpu.SemaphoreType.DMA((2,)),
            pltpu.SemaphoreType.DMA((SENDS,)),
            pltpu.SemaphoreType.DMA((RECEIVES,)),
        ]
        + blocks,
        compiler_params=pltpu.CompilerParams(
            collective_id=0, has_side_effects=True, vmem_limit_bytes=56 * 2**20
        ),
        name="gram_gradient",
    )(view_a, view_b)
    return (moments[1] * left_a).astype(BF16), (moments[3] * left_b).astype(BF16)


def solution(mesh):
    return jax.shard_map(
        body,
        mesh=mesh,
        in_specs=(P("batch", "feat"), P("batch", "feat")),
        out_specs=(P("batch", "feat"), P("batch", "feat")),
        check_vma=False,
    )
```

```python
import functools

import jax
import jax.numpy as jnp
from jax import lax
from jax.experimental import pallas as pl
from jax.experimental.pallas import tpu as pltpu
from jax.sharding import PartitionSpec as P

LAMBDA = 0.0051
MESH = pl.DeviceIdType.MESH
F32 = jnp.float32
BF16 = jnp.bfloat16
SENDS, RECEIVES = 22, 60
REDUCED = (640, 1024, 512)
GATHERED = (640, 1024, 1024)
ROWS = ((0, 1), (16,), (5, 6, 8, 23, 27), (13, 18, 14, 26, 30))
BLOCKS = (
    (1, 0, (2, 3, 7, 11, 17, 21, 36, 42)),
    (0, 0, (4, 10, 15, 22, 39, 45, 51, 56)),
    (1, 1, (9, 12, 19, 24, 28, 33, 40, 54)),
    (1, 2, (29, 34, 38, 43, 47, 50, 55, 59)),
    (0, 1, (20, 25, 31, 37, 44, 48, 53, 58)),
    (0, 2, (32, 35, 41, 46, 49, 52, 57, 60)),
)


def rem4(value):
    return lax.rem(value, 4)


class Net:
    def __init__(self, send_sems, recv_sems):
        self.send_sems, self.recv_sems = send_sems, recv_sems
        self.sends, self.receives = [], 0

    def sender(self, moved):
        self.sends.append(moved)
        return self.send_sems.at[len(self.sends) - 1]

    def receiver(self):
        self.receives += 1
        return self.recv_sems.at[self.receives - 1]

    def finish(self):
        for n, moved in enumerate(self.sends):
            wait(self.send_sems.at[n], moved)


def send(src, dst, sender, receiver, device):
    pltpu.make_async_remote_copy(
        src_ref=src,
        dst_ref=dst,
        send_sem=sender,
        recv_sem=receiver,
        device_id=device,
        device_id_type=MESH,
    ).start()


def wait(sem, moved):
    pltpu.make_async_copy(moved, moved, sem).wait()


def kernel(rows, total, far_a, far_b, ga, gb, moments, *scratch):
    (raw, normed, stat, same, last_a, last_b, acc, cross, back, own, own_sems, send_sems, recv_sems) = scratch[:13]
    blocks = scratch[13:]
    net = Net(send_sems, recv_sems)
    views = (own.at[0], own.at[1])
    loads = [
        pltpu.make_async_copy(source, own.at[v], own_sems.at[v])
        for v, source in enumerate((far_a, far_b))
    ]
    for load in loads:
        load.start()
    batch, feat = lax.axis_index("batch"), lax.axis_index("feat")
    x, core = batch // 2, lax.rem(batch, 2)
    y, z = feat // 4, rem4(feat)

    def at_batch(dx, dcore):
        return (rem4(x + dx) * 2 + lax.rem(core + dcore, 2), feat)

    def at_feat(half, d1, d2):
        dy, dz = (d1, d2) if half == 0 else (d2, d1)
        return (batch, rem4(y + dy) * 4 + rem4(z + dz))

    peers = [(lax.rem(batch + k, 8), feat) for k in (4, 3, 5, 2, 6, 1, 7)]
    planes = [at_feat(half, k, 0) for half in range(2) for k in range(1, 4)]
    barrier = pltpu.get_barrier_semaphore()
    for device in peers + planes:
        pl.semaphore_signal(barrier, inc=1, device_id=device, device_id_type=MESH)

    def sums(step, carry):
        out = []
        for v in range(2):
            values = views[v][pl.ds(pl.multiple_of(step * 64, 64), 64), :].astype(F32)
            out.append(carry[2 * v] + jnp.sum(values.reshape(8, 8, -1), axis=0))
            out.append(carry[2 * v + 1] + jnp.sum((values * values).reshape(8, 8, -1), axis=0))
        return tuple(out)

    zero = jnp.zeros((8, rows), F32)
    for load in loads:
        load.wait()
    parts = lax.fori_loop(0, rows // 64, sums, (zero,) * 4)
    for k in range(4):
        stat[batch, pl.ds(k, 1), :] = jnp.sum(parts[k], axis=0, keepdims=True)
    stat[batch, pl.ds(4, 4), :] = jnp.zeros((4, rows), F32)

    pl.semaphore_wait(barrier, len(peers) + len(planes))

    def exchange(ref, count=8):
        used = pl.ds(0, count)
        sender, receiver = net.sender(ref.at[pl.ds(0, 7), used]), net.receiver()
        for device in peers:
            send(ref.at[batch, used], ref.at[batch, used], sender, receiver, device)
        return receiver

    def collect(ref, receiver, count=8):
        wait(receiver, ref.at[pl.ds(0, 7), pl.ds(0, count)])
        result = ref[0]
        for k in range(1, 8):
            result = result + ref[k]
        return result

    stat_items = exchange(stat, 4)
    sibling = (batch + 1 - 2 * core, feat)
    half = rows // 2
    upper, lower = pl.ds(0, half), pl.ds(half, half)
    view_sends = [net.sender(raw.at[v, pl.ds(0, 7)]) for v in range(2)]
    view_sems = [[net.receiver() for _ in range(7)] for _ in range(2)]

    def send_rows(v, src, slot, device, part=None):
        dst = raw.at[v, slot] if part is None else raw.at[v, slot, part]
        send(src, dst, view_sends[v], view_sems[v][slot - 1], device)

    def wait_rows(v, slot):
        wait(view_sems[v][slot - 1], raw.at[v, slot])

    def send_near(v):
        send_rows(v, views[v], 6, at_batch(1, 0))
        send_rows(v, views[v], 2, at_batch(3, 0))

    send_near(1)
    for v in (1, 0):
        send_rows(v, views[v], 1, sibling)
    send_near(0)

    sum_all = collect(stat, stat_items, 4)
    for v in range(2):
        mean = sum_all[2 * v : 2 * v + 1] / total
        square = sum_all[2 * v + 1 : 2 * v + 2] / total
        moments[pl.ds(2 * v, 1), :] = mean
        moments[pl.ds(2 * v + 1, 1), :] = lax.rsqrt(square - mean * mean + 1e-05)

    def normalize(v, slot):
        source = views[v] if slot == 0 else raw.at[v, slot]

        @pl.loop(0, rows // 64)
        def _(step):
            here = pl.ds(pl.multiple_of(step * 64, 64), 64)
            values = source[here, :].astype(F32)
            unit = (values - moments[pl.ds(2 * v, 1), :]) * moments[pl.ds(2 * v + 1, 1), :]
            normed[v, slot, here, :] = unit.astype(BF16)

    def own_rows(v):
        normalize(v, 0)
        wait_rows(v, 1)
        normalize(v, 1)

    def near_rows(v):
        wait_rows(v, 6)
        wait_rows(v, 2)
        send_rows(v, raw.at[v, 2], 3, sibling)
        send_rows(v, raw.at[v, 6], 7, sibling)

    def take_near(v):
        normalize(v, 2)
        normalize(v, 6)
        for slot in (3, 7):
            wait_rows(v, slot)
            normalize(v, slot)

    def pass_far(v):
        send_rows(v, raw.at[v, 6, upper], 4, at_batch(1, 0), upper)
        send_rows(v, raw.at[v, 2, lower], 4, at_batch(3, 0), lower)

    def far_rows(v):
        wait_rows(v, 4)
        send_rows(v, raw.at[v, 4], 5, sibling)

    def take_far(v):
        normalize(v, 4)
        wait_rows(v, 5)
        normalize(v, 5)

    net.cross_sends = [net.sender(cross.at[v]) for v in range(2)]
    net.back_sends = [net.sender(back.at[v]) for v in range(2)]
    begun = set()

    def cross_rows(part, turn):
        return pl.ds(pl.multiple_of(lax.rem(part + turn, 2) * 256, 256), 256)

    def tile(step):
        return pl.ds(pl.multiple_of(step * 128, 128), 128)

    def partner(step):
        return rem4(step + 2 + (step // 2) * (1 + 2 * lax.rem(step, 2)))

    turned = x // 2

    def mirrored(left, right):
        return lax.dot_general(
            left.reshape(-1, left.shape[-1]), right, (((0,), (0,)), ((), ())), preferred_element_type=F32
        )

    def add(v, here, value):
        acc[v, here, :] = acc[v, here, :] + value if v in begun else value

    class Block:
        def __init__(self, v, kind):
            self.v, self.kind = v, kind
            base = (v * 3 + kind) * 5
            self.part, self.r1, self.r2, self.r3, self.full = blocks[base : base + 5]
            self.cross, self.back = cross.at[v], back.at[v]
            self.columns = REDUCED[kind]
            mirrored = 1 if kind == 2 else 0
            self.reduce_send = net.sender(self.part.at[pl.ds(0, 30)])
            self.gather_send = net.sender(self.full.at[pl.ds(0, 30 + mirrored)])
            self.sems = [net.receiver() for _ in range(7)]

        def mine(self, half):
            return (y, z) if half == 0 else (z, y)

        def product(self):
            v = self.v
            @pl.loop(0, rows // 128)
            def _(step):
                left = normed[v, 0, pl.ds(pl.multiple_of(step * 128, 128), 128), :]

                def block(first, right):
                    value = lax.dot_general(
                        left, right, (((1,), (1,)), ((), ())), preferred_element_type=F32
                    )
                    width = right.shape[0]
                    self.part[pl.ds(step * 8, 8), :, pl.ds(first, width)] = value.astype(
                        BF16
                    ).reshape(8, 16, width)

                if self.kind == 0:
                    block(0, normed[v, 0, cross_rows(step // 2, 0), :])
                    block(256, normed[v, 0, tile(partner(step)), :])
                    block(384, normed[v, 1, cross_rows(step // 2, core), :])
                elif self.kind == 1:
                    block(0, normed[v, 2])
                    block(rows, normed[v, 7])
                else:
                    block(0, normed[v, 4 + turned])

            for half in range(2):
                m1, _ = self.mine(half)
                base = half * 16 + rem4(m1 + 2) * 4
                for k in range(2):
                    send(
                        self.part.at[pl.ds(base + 2 * (1 - k), 2)],
                        self.r1.at[half, k],
                        self.reduce_send,
                        self.sems[0],
                        at_feat(half, 1 + 2 * k, 0),
                    )

        def pass_on(self):
            wait(self.sems[0], self.r1)
            for half in range(2):
                m1, _ = self.mine(half)
                for k in range(2):
                    base = half * 16 + rem4(m1 + 1 + 2 * k) * 4
                    here = pl.ds(base + 2 * (1 - k), 2)
                    self.part[here] = (
                        self.part[here].astype(F32) + self.r1[half, k].astype(F32)
                    ).astype(BF16)
                    send(
                        self.part.at[pl.ds(base, 4)],
                        self.r2.at[half, k],
                        self.reduce_send,
                        self.sems[1],
                        at_feat(half, 1 + 2 * k, 0),
                    )

        def turn(self):
            wait(self.sems[1], self.r2)
            for half in range(2):
                m1, m2 = self.mine(half)
                base = half * 16 + m1 * 4
                here = pl.ds(base, 4)
                self.part[here] = (
                    self.part[here].astype(F32)
                    + self.r2[half, 0].astype(F32)
                    + self.r2[half, 1].astype(F32)
                ).astype(BF16)
                for k in range(1, 4):
                    send(
                        self.part.at[base + rem4(m2 + k)],
                        self.r3.at[half, k - 1],
                        self.reduce_send,
                        self.sems[2],
                        at_feat(half, 0, k),
                    )

        def own(self, half):
            m1, m2 = self.mine(half)
            return half * 16 + m1 * 4 + m2

        def mirror(self, own, first, start, device):
            send(
                self.full.at[own, :, pl.ds(first, 512)],
                self.full.at[own, :, pl.ds(start, 512)],
                self.gather_send,
                self.sems[3],
                device,
            )

        def reduced(self):
            wait(self.sems[2], self.r3)
            for half in range(2):
                own = self.own(half)
                value = self.part[own].astype(F32)
                for k in range(3):
                    value = value + self.r3[half, k].astype(F32)
                self.full[own, :, pl.ds(0, self.columns)] = value.astype(BF16)
                if self.kind == 2:
                    self.mirror(own, 0, 512, at_batch(2, turned))
            if self.kind != 2:
                self.spread()

        def spread(self):
            if self.kind == 2:
                wait(self.sems[3], self.full.at[pl.ds(0, 1)])
            for half in range(2):
                here = self.full.at[self.own(half)]
                for k in range(1, 4):
                    send(here, here, self.gather_send, self.sems[4], at_feat(half, 0, k))

        def send_back(self, half, ahead, first, count):
            m1, _ = self.mine(half)
            chunks = pl.ds(half * 16 + rem4(m1 + ahead) * 4 + first, count)
            for k, device in enumerate((at_batch(1, 0), at_batch(3, 1))):
                send(
                    self.full.at[chunks, :, pl.ds(512 * k, 512)],
                    self.back.at[k, chunks],
                    net.back_sends[self.v],
                    self.sems[3],
                    device,
                )

        def gather(self):
            wait(self.sems[4], self.full.at[pl.ds(0, 6)])
            for half in range(2):
                m1, _ = self.mine(half)
                here = self.full.at[pl.ds(half * 16 + m1 * 4, 4)]
                for k in range(2):
                    send(here, here, self.gather_send, self.sems[5], at_feat(half, 1 + 2 * k, 0))
                if self.kind == 1:
                    self.send_back(half, 0, 0, 4)

        def gather_on(self):
            wait(self.sems[5], self.full.at[pl.ds(0, 16)])
            for half in range(2):
                m1, _ = self.mine(half)
                for k in range(2):
                    base = half * 16 + rem4(m1 + 3 + 2 * k) * 4
                    here = self.full.at[pl.ds(base + 2 * k, 2)]
                    send(here, here, self.gather_send, self.sems[6], at_feat(half, 1 + 2 * k, 0))
                    if self.kind == 1:
                        self.send_back(half, 3 + 2 * k, 0, 4)

        def arrived(self):
            wait(self.sems[6], self.full.at[pl.ds(0, 8)])
            if self.kind == 1:
                for half in range(2):
                    self.send_back(half, 2, 0, 4)

        def swap(self):
            self.arrived()
            send(
                self.full.at[:, :, pl.ds(384, 256)],
                self.cross,
                net.cross_sends[self.v],
                self.sems[3],
                sibling,
            )

        def apply(self):
            if self.kind == 0:
                wait(self.sems[3], self.cross)
            else:
                self.arrived()
            other = 1 - self.v
            if self.kind == 0:
                self.apply_own(other)
            else:

                @pl.loop(0, 2)
                def _(step):
                    here = pl.ds(pl.multiple_of(step * 256, 256), 256)

                    def direct(first, right):
                        left = self.full[pl.ds(step * 16, 16), :, pl.ds(first, 512)]
                        return jnp.dot(
                            left.reshape(256, 512), right, preferred_element_type=F32
                        )

                    if self.kind == 1:
                        value = direct(0, normed[other, 2]) + direct(rows, normed[other, 7])
                    else:
                        value = direct(0, normed[other, 4 + turned])
                        columns = pl.ds(pl.multiple_of(512 + step * 256, 256), 256)
                        left = self.full[:, :, columns]
                        value += mirrored(left, normed[other, 5 - turned])
                    add(other, here, value)

            begun.add(other)

        def apply_own(self, other):
            @pl.loop(0, rows // 128)
            def _(step):
                here = pl.ds(pl.multiple_of(step * 128, 128), 128)

                def direct(first, right):
                    width = right.shape[0]
                    left = self.full[pl.ds(step * 8, 8), :, pl.ds(first, width)]
                    return jnp.dot(
                        left.reshape(128, width), right, preferred_element_type=F32
                    )

                value = direct(0, normed[other, 0, cross_rows(step // 2, 0), :])
                value += direct(256, normed[other, 0, tile(partner(step)), :])
                value += direct(384, normed[other, 1, cross_rows(step // 2, core), :])
                taker = 3 - step + (step // 2) * (2 * step - 5)
                left = self.full[pl.ds(taker * 8, 8), :, pl.ds(256, 128)]
                value += mirrored(left, normed[other, 0, tile(taker), :])
                theirs = lax.rem(step // 2 + 1 - core, 2)
                first = pl.multiple_of(lax.rem(step, 2) * 128, 128)
                left = self.cross[pl.ds(theirs * 16, 16), :, pl.ds(first, 128)]
                value += mirrored(left, normed[other, 1, cross_rows(theirs, 0), :])
                add(other, here, value)

        def apply_back(self):
            wait(self.sems[3], self.back)
            other = 1 - self.v

            @pl.loop(0, 2)
            def _(step):
                here = pl.ds(pl.multiple_of(step * 256, 256), 256)
                value = mirrored(self.back[0, :, :, here], normed[other, 6])
                value += mirrored(self.back[1, :, :, here], normed[other, 3])
                add(other, here, value)

            begun.add(other)

        def stages(self):
            reduce = [self.product, self.pass_on, self.turn, self.reduced]
            if self.kind == 0:
                return reduce + [self.gather, self.gather_on, self.swap, self.apply]
            if self.kind == 1:
                return reduce + [self.gather, self.gather_on, self.apply, self.apply_back]
            return reduce + [self.spread, self.gather, self.gather_on, self.apply]

    same_items = []
    extras = []

    def diagonal():
        def step_sum(step, carry):
            here = pl.ds(pl.multiple_of(step * 64, 64), 64)
            both = normed[0, 0, here, :].astype(F32) * normed[1, 0, here, :].astype(F32)
            return carry + jnp.sum(both.reshape(8, 8, -1), axis=0)

        part = lax.fori_loop(0, rows // 64, step_sum, zero)
        same[batch] = part
        same_items.append(exchange(same))

    def unit_of(v, here):
        values = views[v][here, :].astype(F32)
        return (values - moments[pl.ds(2 * v, 1), :]) * moments[pl.ds(2 * v + 1, 1), :]

    def back_sums(v, last):
        def step_sum(step, carry):
            here = pl.ds(pl.multiple_of(step * 64, 64), 64)
            back = (2.0 * LAMBDA / total) * acc[v, here, :]
            back += extras[0] * normed[1 - v, 0, here, :].astype(F32)
            acc[v, here, :] = back
            first = carry[0] + jnp.sum(back.reshape(8, 8, -1), axis=0)
            second = carry[1] + jnp.sum((back * unit_of(v, here)).reshape(8, 8, -1), axis=0)
            return first, second

        first, second = lax.fori_loop(0, rows // 64, step_sum, (zero, zero))
        last[batch, pl.ds(0, 1), :] = jnp.sum(first, axis=0, keepdims=True)
        last[batch, pl.ds(1, 1), :] = jnp.sum(second, axis=0, keepdims=True)
        last[batch, pl.ds(2, 6), :] = jnp.zeros((6, rows), F32)
        return exchange(last, 2)

    def finish(v, last, items, out):
        both = collect(last, items, 2) / total
        first, second = both[0:1], both[1:2]

        @pl.loop(0, rows // 64)
        def _(step):
            here = pl.ds(pl.multiple_of(step * 64, 64), 64)
            out[here, :] = acc[v, here, :] - first - unit_of(v, here) * second

    plan = []

    def add_rows(name, ticks):
        plan.extend(zip(ticks, name))

    add_rows([lambda v=v: own_rows(v) for v in (1, 0)], ROWS[0])
    add_rows([diagonal], ROWS[1])
    for n, v in enumerate((1, 0)):
        steps = [lambda v=v, f=f: f(v) for f in (near_rows, take_near, pass_far, far_rows, take_far)]
        add_rows(steps, ROWS[2 + n])
    for v, kind, ticks in BLOCKS:
        add_rows(Block(v, kind).stages(), ticks)
    def early():
        cosine = jnp.sum(collect(same, same_items[0]), axis=0, keepdims=True) / total
        extra = (2.0 * (cosine - 1.0)).astype(BF16).astype(F32) - 2.0 * LAMBDA * cosine
        extras.append(extra)
        extras.append(back_sums(0, last_a))

    add_rows([early], (max(ticks[-1] for v, _, ticks in BLOCKS if v == 1),))
    for _, step in sorted(plan, key=lambda item: item[0]):
        step()
    items_b = back_sums(1, last_b)
    finish(0, last_a, extras[1], ga)
    finish(1, last_b, items_b, gb)
    net.finish()
    assert (len(net.sends), net.receives) == (SENDS, RECEIVES)


def body(view_a, view_b):
    rows, width = view_a.shape
    total = rows * lax.axis_size("batch")
    blocks = []
    for _ in range(2):
        for columns, wide in zip(REDUCED, GATHERED):
            blocks += [
                pltpu.VMEM((32, 16, columns), BF16),
                pltpu.VMEM((2, 2, 2, 16, columns), BF16),
                pltpu.VMEM((2, 2, 4, 16, columns), BF16),
                pltpu.VMEM((2, 3, 16, columns), BF16),
                pltpu.VMEM((32, 16, wide), BF16),
            ]
    vmem = pl.BlockSpec(memory_space=pltpu.VMEM)
    left_a, left_b, moments = pl.pallas_call(
        functools.partial(kernel, rows, total),
        out_shape=(pltpu.VMEM((rows, width), F32),) * 2 + (pltpu.VMEM((8, width), F32),),
        in_specs=[pl.BlockSpec(memory_space=pl.ANY)] * 2,
        out_specs=(vmem, vmem, vmem),
        scratch_shapes=[
            pltpu.VMEM((2, 8, rows, width), BF16),
            pltpu.VMEM((2, 8, rows, width), BF16),
            pltpu.VMEM((8, 8, width), F32),
            pltpu.VMEM((8, 8, width), F32),
            pltpu.VMEM((8, 8, width), F32),
            pltpu.VMEM((8, 8, width), F32),
            pltpu.VMEM((2, rows, width), F32),
            pltpu.VMEM((2, 32, 16, 256), BF16),
            pltpu.VMEM((2, 2, 32, 16, 512), BF16),
            pltpu.VMEM((2, rows, width), BF16),
            pltpu.SemaphoreType.DMA((2,)),
            pltpu.SemaphoreType.DMA((SENDS,)),
            pltpu.SemaphoreType.DMA((RECEIVES,)),
        ]
        + blocks,
        compiler_params=pltpu.CompilerParams(
            collective_id=0, has_side_effects=True, vmem_limit_bytes=56 * 2**20
        ),
        name="gram_gradient",
    )(view_a, view_b)
    return (moments[1] * left_a).astype(BF16), (moments[3] * left_b).astype(BF16)


def solution(mesh):
    return jax.shard_map(
        body,
        mesh=mesh,
        in_specs=(P("batch", "feat"), P("batch", "feat")),
        out_specs=(P("batch", "feat"), P("batch", "feat")),
        check_vma=False,
    )
```

```python
import functools

import jax
import jax.numpy as jnp
from jax import lax
from jax.experimental import pallas as pl
from jax.experimental.pallas import tpu as pltpu
from jax.sharding import PartitionSpec as P

LAMBDA = 0.0051
MESH = pl.DeviceIdType.MESH
F32 = jnp.float32
BF16 = jnp.bfloat16
SENDS, RECEIVES = 22, 60
REDUCED = (640, 1024, 512)
GATHERED = (640, 1024, 1024)
ROWS = ((0, 1), (16,), (5, 6, 8, 23, 27), (13, 18, 14, 26, 30))
BLOCKS = (
    (1, 0, (2, 3, 7, 11, 17, 21, 36, 42)),
    (0, 0, (4, 10, 15, 22, 39, 45, 51, 56)),
    (1, 1, (9, 12, 19, 24, 28, 33, 40, 54)),
    (1, 2, (29, 34, 38, 43, 47, 50, 55, 59)),
    (0, 1, (20, 25, 31, 37, 44, 48, 53, 58)),
    (0, 2, (32, 35, 41, 46, 49, 52, 57, 60)),
)


def rem4(value):
    return lax.rem(value, 4)


class Net:
    def __init__(self, send_sems, recv_sems):
        self.send_sems, self.recv_sems = send_sems, recv_sems
        self.sends, self.receives = [], 0

    def sender(self, moved):
        self.sends.append(moved)
        return self.send_sems.at[len(self.sends) - 1]

    def receiver(self):
        self.receives += 1
        return self.recv_sems.at[self.receives - 1]

    def finish(self):
        for n, moved in enumerate(self.sends):
            wait(self.send_sems.at[n], moved)


def send(src, dst, sender, receiver, device):
    pltpu.make_async_remote_copy(
        src_ref=src,
        dst_ref=dst,
        send_sem=sender,
        recv_sem=receiver,
        device_id=device,
        device_id_type=MESH,
    ).start()


def wait(sem, moved):
    pltpu.make_async_copy(moved, moved, sem).wait()


def kernel(rows, total, far_a, far_b, acc_a, acc_b, moments, sums_ab, *scratch):
    (raw, normed, stat, same, last_a, last_b, cross, mirror, own, row_sums, own_sems, send_sems, recv_sems) = scratch[:13]
    blocks = scratch[13:]
    acc = (acc_a, acc_b)
    net = Net(send_sems, recv_sems)
    views = (own.at[0], own.at[1])
    loads = [
        pltpu.make_async_copy(source, own.at[v], own_sems.at[v])
        for v, source in enumerate((far_a, far_b))
    ]
    for load in loads:
        load.start()
    batch, feat = lax.axis_index("batch"), lax.axis_index("feat")
    x, core = batch // 2, lax.rem(batch, 2)
    y, z = feat // 4, rem4(feat)

    def at_batch(dx, dcore):
        return (rem4(x + dx) * 2 + lax.rem(core + dcore, 2), feat)

    def at_feat(half, d1, d2):
        dy, dz = (d1, d2) if half == 0 else (d2, d1)
        return (batch, rem4(y + dy) * 4 + rem4(z + dz))

    peers = [(lax.rem(batch + k, 8), feat) for k in (4, 3, 5, 2, 6, 1, 7)]
    planes = [at_feat(half, k, 0) for half in range(2) for k in (2, 1, 3)]
    barrier = pltpu.get_barrier_semaphore()
    for device in peers + planes:
        pl.semaphore_signal(barrier, inc=1, device_id=device, device_id_type=MESH)

    def sums(step, carry):
        out = []
        for v in range(2):
            values = views[v][pl.ds(pl.multiple_of(step * 64, 64), 64), :].astype(F32)
            out.append(carry[2 * v] + jnp.sum(values.reshape(8, 8, -1), axis=0))
            out.append(carry[2 * v + 1] + jnp.sum((values * values).reshape(8, 8, -1), axis=0))
        return tuple(out)

    zero = jnp.zeros((8, rows), F32)
    for load in loads:
        load.wait()
    parts = lax.fori_loop(0, rows // 64, sums, (zero,) * 4)
    for k in range(4):
        stat[batch, pl.ds(k, 1), :] = jnp.sum(parts[k], axis=0, keepdims=True)
    stat[batch, pl.ds(4, 4), :] = jnp.zeros((4, rows), F32)

    pl.semaphore_wait(barrier, len(peers) + len(planes))

    def exchange(ref, count=8):
        used = pl.ds(0, count)
        sender, receiver = net.sender(ref.at[pl.ds(0, 7), used]), net.receiver()
        for device in peers:
            send(ref.at[batch, used], ref.at[batch, used], sender, receiver, device)
        return receiver

    def collect(ref, receiver, count=8):
        wait(receiver, ref.at[pl.ds(0, 7), pl.ds(0, count)])
        result = ref[0]
        for k in range(1, 8):
            result = result + ref[k]
        return result

    stat_items = exchange(stat, 4)
    sibling = (batch + 1 - 2 * core, feat)
    half = rows // 2
    upper, lower = pl.ds(0, half), pl.ds(half, half)
    view_sends = [net.sender(raw.at[v, pl.ds(0, 7)]) for v in range(2)]
    view_sems = [[net.receiver() for _ in range(7)] for _ in range(2)]

    def send_rows(v, src, slot, device, part=None):
        dst = raw.at[v, slot] if part is None else raw.at[v, slot, part]
        send(src, dst, view_sends[v], view_sems[v][slot - 1], device)

    def wait_rows(v, slot):
        wait(view_sems[v][slot - 1], raw.at[v, slot])

    def send_near(v):
        send_rows(v, views[v], 6, at_batch(1, 0))
        send_rows(v, views[v], 2, at_batch(3, 0))

    send_near(1)
    for v in (1, 0):
        send_rows(v, views[v], 1, sibling)
    send_near(0)

    sum_all = collect(stat, stat_items, 4)
    for v in range(2):
        mean = sum_all[2 * v : 2 * v + 1] / total
        square = sum_all[2 * v + 1 : 2 * v + 2] / total
        moments[pl.ds(2 * v, 1), :] = mean
        moments[pl.ds(2 * v + 1, 1), :] = lax.rsqrt(square - mean * mean + 1e-05)

    def normalize(v, slot):
        source = views[v] if slot == 0 else raw.at[v, slot]

        @pl.loop(0, rows // 64)
        def _(step):
            here = pl.ds(pl.multiple_of(step * 64, 64), 64)
            values = source[here, :].astype(F32)
            unit = (values - moments[pl.ds(2 * v, 1), :]) * moments[pl.ds(2 * v + 1, 1), :]
            normed[v, slot, here, :] = unit.astype(BF16)

    def own_rows(v):
        normalize(v, 0)
        wait_rows(v, 1)
        normalize(v, 1)

    def near_rows(v):
        wait_rows(v, 6)
        wait_rows(v, 2)
        send_rows(v, raw.at[v, 2], 3, sibling)
        send_rows(v, raw.at[v, 6], 7, sibling)

    def take_near(v):
        normalize(v, 2)
        normalize(v, 6)
        for slot in (3, 7):
            wait_rows(v, slot)
            normalize(v, slot)

    def pass_far(v):
        send_rows(v, raw.at[v, 6, upper], 4, at_batch(1, 0), upper)
        send_rows(v, raw.at[v, 2, lower], 4, at_batch(3, 0), lower)

    def far_rows(v):
        wait_rows(v, 4)
        send_rows(v, raw.at[v, 4], 5, sibling)

    def take_far(v):
        normalize(v, 4)
        wait_rows(v, 5)
        normalize(v, 5)

    net.cross_sends = [net.sender(cross.at[v]) for v in range(2)]
    net.back_sends = [net.sender(mirror.at[v]) for v in range(2)]
    added = [0, 0]
    row_sums[...] = jnp.zeros((2, 8, rows), F32)

    def cross_rows(part, turn):
        return pl.ds(pl.multiple_of(lax.rem(part + turn, 2) * 256, 256), 256)

    def tile(step):
        return pl.ds(pl.multiple_of(step * 128, 128), 128)

    def partner(step):
        return rem4(step + 2 + (step // 2) * (1 + 2 * lax.rem(step, 2)))

    turned = x // 2

    def mirrored(left, right):
        return lax.dot_general(
            left.reshape(-1, left.shape[-1]), right, (((0,), (0,)), ((), ())), preferred_element_type=F32
        )

    def add(v, here, value):
        if added[v] < 3 or v == 0:
            acc[v][here, :] = acc[v][here, :] + value if added[v] else value
            return
        back = (2.0 * LAMBDA / total) * (acc[v][here, :] + value)
        back += extras[0] * normed[1 - v, 0, here, :].astype(F32)
        acc[v][here, :] = back
        row_sums[0] += jnp.sum(back.reshape(-1, 8, rows), axis=0)
        row_sums[1] += jnp.sum((back * unit_of(v, here)).reshape(-1, 8, rows), axis=0)

    class Block:
        def __init__(self, v, kind):
            self.v, self.kind = v, kind
            base = (v * 3 + kind) * 5
            self.part, self.r1, self.r2, self.r3, self.full = blocks[base : base + 5]
            self.cross, self.back = cross.at[v], mirror.at[v]
            self.columns = REDUCED[kind]
            mirrored = 1 if kind == 2 else 0
            self.reduce_send = net.sender(self.part.at[pl.ds(0, 30)])
            self.gather_send = net.sender(self.full.at[pl.ds(0, 30 + mirrored)])
            self.sems = [net.receiver() for _ in range(7)]

        def mine(self, half):
            return (y, z) if half == 0 else (z, y)

        def product(self):
            v = self.v
            @pl.loop(0, rows // 128)
            def _(step):
                left = normed[v, 0, pl.ds(pl.multiple_of(step * 128, 128), 128), :]

                def block(first, right):
                    value = lax.dot_general(
                        left, right, (((1,), (1,)), ((), ())), preferred_element_type=F32
                    )
                    width = right.shape[0]
                    self.part[pl.ds(step * 8, 8), :, pl.ds(first, width)] = value.astype(
                        BF16
                    ).reshape(8, 16, width)

                if self.kind == 0:
                    block(0, normed[v, 0, cross_rows(step // 2, 0), :])
                    block(256, normed[v, 0, tile(partner(step)), :])
                    block(384, normed[v, 1, cross_rows(step // 2, core), :])
                elif self.kind == 1:
                    block(0, normed[v, 2])
                    block(rows, normed[v, 7])
                else:
                    block(0, normed[v, 4 + turned])

            for half in range(2):
                m1, _ = self.mine(half)
                base = half * 16 + rem4(m1 + 2) * 4
                for k in range(2):
                    send(
                        self.part.at[pl.ds(base + 2 * (1 - k), 2)],
                        self.r1.at[half, k],
                        self.reduce_send,
                        self.sems[0],
                        at_feat(half, 1 + 2 * k, 0),
                    )

        def pass_on(self):
            wait(self.sems[0], self.r1)
            for half in range(2):
                m1, _ = self.mine(half)
                for k in range(2):
                    base = half * 16 + rem4(m1 + 1 + 2 * k) * 4
                    here = pl.ds(base + 2 * (1 - k), 2)
                    self.part[here] = (
                        self.part[here].astype(F32) + self.r1[half, k].astype(F32)
                    ).astype(BF16)
                    send(
                        self.part.at[pl.ds(base, 4)],
                        self.r2.at[half, k],
                        self.reduce_send,
                        self.sems[1],
                        at_feat(half, 1 + 2 * k, 0),
                    )

        def turn(self):
            wait(self.sems[1], self.r2)
            for half in range(2):
                m1, m2 = self.mine(half)
                base = half * 16 + m1 * 4
                here = pl.ds(base, 4)
                self.part[here] = (
                    self.part[here].astype(F32)
                    + self.r2[half, 0].astype(F32)
                    + self.r2[half, 1].astype(F32)
                ).astype(BF16)
                for k in range(1, 4):
                    send(
                        self.part.at[base + rem4(m2 + k)],
                        self.r3.at[half, k - 1],
                        self.reduce_send,
                        self.sems[2],
                        at_feat(half, 0, k),
                    )

        def own(self, half):
            m1, m2 = self.mine(half)
            return half * 16 + m1 * 4 + m2

        def mirror(self, own, first, start, device):
            send(
                self.full.at[own, :, pl.ds(first, 512)],
                self.full.at[own, :, pl.ds(start, 512)],
                self.gather_send,
                self.sems[3],
                device,
            )

        def reduced(self):
            wait(self.sems[2], self.r3)
            for half in range(2):
                own = self.own(half)
                value = self.part[own].astype(F32)
                for k in range(3):
                    value = value + self.r3[half, k].astype(F32)
                self.full[own, :, pl.ds(0, self.columns)] = value.astype(BF16)
                if self.kind == 2:
                    self.mirror(own, 0, 512, at_batch(2, turned))
            if self.kind != 2:
                self.spread()

        def spread(self):
            if self.kind == 2:
                wait(self.sems[3], self.full.at[pl.ds(0, 1)])
            for half in range(2):
                here = self.full.at[self.own(half)]
                for k in range(1, 4):
                    send(here, here, self.gather_send, self.sems[4], at_feat(half, 0, k))

        def send_back(self, half, ahead, first, count):
            m1, _ = self.mine(half)
            chunks = pl.ds(half * 16 + rem4(m1 + ahead) * 4 + first, count)
            for k, device in enumerate((at_batch(1, 0), at_batch(3, 1))):
                send(
                    self.full.at[chunks, :, pl.ds(512 * k, 512)],
                    self.back.at[k, chunks],
                    net.back_sends[self.v],
                    self.sems[3],
                    device,
                )

        def gather(self):
            wait(self.sems[4], self.full.at[pl.ds(0, 6)])
            for half in range(2):
                m1, _ = self.mine(half)
                here = self.full.at[pl.ds(half * 16 + m1 * 4, 4)]
                for k in range(2):
                    send(here, here, self.gather_send, self.sems[5], at_feat(half, 1 + 2 * k, 0))
                if self.kind == 1:
                    self.send_back(half, 0, 0, 4)

        def gather_on(self):
            wait(self.sems[5], self.full.at[pl.ds(0, 16)])
            for half in range(2):
                m1, _ = self.mine(half)
                for k in range(2):
                    base = half * 16 + rem4(m1 + 3 + 2 * k) * 4
                    here = self.full.at[pl.ds(base + 2 * k, 2)]
                    send(here, here, self.gather_send, self.sems[6], at_feat(half, 1 + 2 * k, 0))
                    if self.kind == 1:
                        self.send_back(half, 3 + 2 * k, 0, 4)

        def arrived(self):
            wait(self.sems[6], self.full.at[pl.ds(0, 8)])
            if self.kind == 1:
                for half in range(2):
                    self.send_back(half, 2, 0, 4)

        def swap(self):
            self.arrived()
            send(
                self.full.at[:, :, pl.ds(384, 256)],
                self.cross,
                net.cross_sends[self.v],
                self.sems[3],
                sibling,
            )

        def apply(self):
            if self.kind == 0:
                wait(self.sems[3], self.cross)
            else:
                self.arrived()
            other = 1 - self.v
            if self.kind == 0:
                self.apply_own(other)
            else:

                @pl.loop(0, 2)
                def _(step):
                    here = pl.ds(pl.multiple_of(step * 256, 256), 256)

                    def direct(first, right):
                        left = self.full[pl.ds(step * 16, 16), :, pl.ds(first, 512)]
                        return jnp.dot(
                            left.reshape(256, 512), right, preferred_element_type=F32
                        )

                    if self.kind == 1:
                        value = direct(0, normed[other, 2]) + direct(rows, normed[other, 7])
                    else:
                        value = direct(0, normed[other, 4 + turned])
                        columns = pl.ds(pl.multiple_of(512 + step * 256, 256), 256)
                        left = self.full[:, :, columns]
                        value += mirrored(left, normed[other, 5 - turned])
                    add(other, here, value)

            added[other] += 1

        def apply_own(self, other):
            @pl.loop(0, rows // 128)
            def _(step):
                here = pl.ds(pl.multiple_of(step * 128, 128), 128)

                def direct(first, right):
                    width = right.shape[0]
                    left = self.full[pl.ds(step * 8, 8), :, pl.ds(first, width)]
                    return jnp.dot(
                        left.reshape(128, width), right, preferred_element_type=F32
                    )

                value = direct(0, normed[other, 0, cross_rows(step // 2, 0), :])
                value += direct(256, normed[other, 0, tile(partner(step)), :])
                value += direct(384, normed[other, 1, cross_rows(step // 2, core), :])
                taker = 3 - step + (step // 2) * (2 * step - 5)
                left = self.full[pl.ds(taker * 8, 8), :, pl.ds(256, 128)]
                value += mirrored(left, normed[other, 0, tile(taker), :])
                theirs = lax.rem(step // 2 + 1 - core, 2)
                first = pl.multiple_of(lax.rem(step, 2) * 128, 128)
                left = self.cross[pl.ds(theirs * 16, 16), :, pl.ds(first, 128)]
                value += mirrored(left, normed[other, 1, cross_rows(theirs, 0), :])
                add(other, here, value)

        def apply_back(self):
            wait(self.sems[3], self.back)
            other = 1 - self.v

            @pl.loop(0, 2)
            def _(step):
                here = pl.ds(pl.multiple_of(step * 256, 256), 256)
                value = mirrored(self.back[0, :, :, here], normed[other, 6])
                value += mirrored(self.back[1, :, :, here], normed[other, 3])
                add(other, here, value)

            added[other] += 1

        def stages(self):
            reduce = [self.product, self.pass_on, self.turn, self.reduced]
            if self.kind == 0:
                return reduce + [self.gather, self.gather_on, self.swap, self.apply]
            if self.kind == 1:
                return reduce + [self.gather, self.gather_on, self.apply, self.apply_back]
            return reduce + [self.spread, self.gather, self.gather_on, self.apply]

    same_items = []
    extras = []

    def diagonal():
        def step_sum(step, carry):
            here = pl.ds(pl.multiple_of(step * 64, 64), 64)
            both = normed[0, 0, here, :].astype(F32) * normed[1, 0, here, :].astype(F32)
            return carry + jnp.sum(both.reshape(8, 8, -1), axis=0)

        part = lax.fori_loop(0, rows // 64, step_sum, zero)
        same[batch] = part
        same_items.append(exchange(same))

    def unit_of(v, here):
        values = views[v][here, :].astype(F32)
        return (values - moments[pl.ds(2 * v, 1), :]) * moments[pl.ds(2 * v + 1, 1), :]

    def back_sums(v, last):
        def step_sum(step, carry):
            here = pl.ds(pl.multiple_of(step * 64, 64), 64)
            back = (2.0 * LAMBDA / total) * acc[v][here, :]
            back += extras[0] * normed[1 - v, 0, here, :].astype(F32)
            acc[v][here, :] = back
            first = carry[0] + jnp.sum(back.reshape(8, 8, -1), axis=0)
            second = carry[1] + jnp.sum((back * unit_of(v, here)).reshape(8, 8, -1), axis=0)
            return first, second

        first, second = lax.fori_loop(0, rows // 64, step_sum, (zero, zero))
        return send_sums(first, second, last)

    def send_sums(first, second, last):
        last[batch, pl.ds(0, 1), :] = jnp.sum(first, axis=0, keepdims=True)
        last[batch, pl.ds(1, 1), :] = jnp.sum(second, axis=0, keepdims=True)
        last[batch, pl.ds(2, 6), :] = jnp.zeros((6, rows), F32)
        return exchange(last, 2)

    def finish(v, last, items):
        sums_ab[pl.ds(2 * v, 2), :] = (collect(last, items, 2) / total)[0:2]

    plan = []

    def add_rows(name, ticks):
        plan.extend(zip(ticks, name))

    add_rows([lambda v=v: own_rows(v) for v in (1, 0)], ROWS[0])
    add_rows([diagonal], ROWS[1])
    for n, v in enumerate((1, 0)):
        steps = [lambda v=v, f=f: f(v) for f in (near_rows, take_near, pass_far, far_rows, take_far)]
        add_rows(steps, ROWS[2 + n])
    for v, kind, ticks in BLOCKS:
        add_rows(Block(v, kind).stages(), ticks)
    def early():
        cosine = jnp.sum(collect(same, same_items[0]), axis=0, keepdims=True) / total
        extra = (2.0 * (cosine - 1.0)).astype(BF16).astype(F32) - 2.0 * LAMBDA * cosine
        extras.append(extra)
        extras.append(back_sums(0, last_a))

    add_rows([early], (max(ticks[-1] for v, _, ticks in BLOCKS if v == 1),))
    for _, step in sorted(plan, key=lambda item: item[0]):
        step()
    assert added == [4, 4]
    items_b = send_sums(row_sums[0], row_sums[1], last_b)
    sums_ab[pl.ds(4, 4), :] = jnp.zeros((4, rows), F32)
    finish(0, last_a, extras[1])
    finish(1, last_b, items_b)
    net.finish()
    assert (len(net.sends), net.receives) == (SENDS, RECEIVES)


def body(view_a, view_b):
    rows, width = view_a.shape
    total = rows * lax.axis_size("batch")
    blocks = []
    for _ in range(2):
        for columns, wide in zip(REDUCED, GATHERED):
            blocks += [
                pltpu.VMEM((32, 16, columns), BF16),
                pltpu.VMEM((2, 2, 2, 16, columns), BF16),
                pltpu.VMEM((2, 2, 4, 16, columns), BF16),
                pltpu.VMEM((2, 3, 16, columns), BF16),
                pltpu.VMEM((32, 16, wide), BF16),
            ]
    vmem = pl.BlockSpec(memory_space=pltpu.VMEM)
    back_a, back_b, moments, sums = pl.pallas_call(
        functools.partial(kernel, rows, total),
        out_shape=(pltpu.VMEM((rows, width), F32),) * 2 + (pltpu.VMEM((8, width), F32),) * 2,
        in_specs=[pl.BlockSpec(memory_space=pl.ANY)] * 2,
        out_specs=(vmem,) * 4,
        scratch_shapes=[
            pltpu.VMEM((2, 8, rows, width), BF16),
            pltpu.VMEM((2, 8, rows, width), BF16),
            pltpu.VMEM((8, 8, width), F32),
            pltpu.VMEM((8, 8, width), F32),
            pltpu.VMEM((8, 8, width), F32),
            pltpu.VMEM((8, 8, width), F32),
            pltpu.VMEM((2, 32, 16, 256), BF16),
            pltpu.VMEM((2, 2, 32, 16, 512), BF16),
            pltpu.VMEM((2, rows, width), BF16),
            pltpu.VMEM((2, 8, width), F32),
            pltpu.SemaphoreType.DMA((2,)),
            pltpu.SemaphoreType.DMA((SENDS,)),
            pltpu.SemaphoreType.DMA((RECEIVES,)),
        ]
        + blocks,
        compiler_params=pltpu.CompilerParams(
            collective_id=0, has_side_effects=True, vmem_limit_bytes=56 * 2**20
        ),
        name="gram_gradient",
    )(view_a, view_b)

    def gradient(v, view, back):
        scale = moments[2 * v + 1]
        unit = (view.astype(F32) - moments[2 * v]) * scale
        return (scale * (back - sums[2 * v] - unit * sums[2 * v + 1])).astype(BF16)

    return gradient(0, view_a, back_a), gradient(1, view_b, back_b)


def solution(mesh):
    return jax.shard_map(
        body,
        mesh=mesh,
        in_specs=(P("batch", "feat"), P("batch", "feat")),
        out_specs=(P("batch", "feat"), P("batch", "feat")),
        check_vma=False,
    )
```

```python
import functools

import jax
import jax.numpy as jnp
from jax import lax
from jax.experimental import pallas as pl
from jax.experimental.pallas import tpu as pltpu
from jax.sharding import PartitionSpec as P

LAMBDA = 0.0051
MESH = pl.DeviceIdType.MESH
F32 = jnp.float32
BF16 = jnp.bfloat16
SENDS, RECEIVES = 22, 60
REDUCED = (640, 1024, 512)
GATHERED = (640, 1024, 1024)
ROWS = ((0, 1), (16,), (5, 6, 8, 23, 27), (13, 18, 14, 26, 30))
BLOCKS = (
    (1, 0, (2, 3, 7, 11, 17, 21, 36, 42)),
    (0, 0, (4, 10, 15, 22, 39, 45, 51, 56)),
    (1, 1, (9, 12, 19, 24, 28, 33, 40, 54)),
    (1, 2, (29, 34, 38, 43, 47, 50, 55, 59)),
    (0, 1, (20, 25, 31, 37, 44, 48, 53, 58)),
    (0, 2, (32, 35, 41, 46, 49, 52, 57, 60)),
)


def rem4(value):
    return lax.rem(value, 4)


class Net:
    def __init__(self, send_sems, recv_sems):
        self.send_sems, self.recv_sems = send_sems, recv_sems
        self.sends, self.receives = [], 0

    def sender(self, moved):
        self.sends.append(moved)
        return self.send_sems.at[len(self.sends) - 1]

    def receiver(self):
        self.receives += 1
        return self.recv_sems.at[self.receives - 1]

    def finish(self):
        for n, moved in enumerate(self.sends):
            wait(self.send_sems.at[n], moved)


def send(src, dst, sender, receiver, device):
    pltpu.make_async_remote_copy(
        src_ref=src,
        dst_ref=dst,
        send_sem=sender,
        recv_sem=receiver,
        device_id=device,
        device_id_type=MESH,
    ).start()


def wait(sem, moved):
    pltpu.make_async_copy(moved, moved, sem).wait()


def kernel(rows, total, far_a, far_b, ga, gb, moments, *scratch):
    (raw, normed, stat, same, last_a, last_b, acc, cross, back, own, own_sems, send_sems, recv_sems) = scratch[:13]
    blocks = scratch[13:]
    net = Net(send_sems, recv_sems)
    views = (own.at[0], own.at[1])
    loads = [
        pltpu.make_async_copy(source, own.at[v], own_sems.at[v])
        for v, source in enumerate((far_a, far_b))
    ]
    for load in loads:
        load.start()
    batch, feat = lax.axis_index("batch"), lax.axis_index("feat")
    x, core = batch // 2, lax.rem(batch, 2)
    y, z = feat // 4, rem4(feat)

    def at_batch(dx, dcore):
        return (rem4(x + dx) * 2 + lax.rem(core + dcore, 2), feat)

    def at_feat(half, d1, d2):
        dy, dz = (d1, d2) if half == 0 else (d2, d1)
        return (batch, rem4(y + dy) * 4 + rem4(z + dz))

    peers = [(lax.rem(batch + k, 8), feat) for k in (4, 3, 5, 2, 6, 1, 7)]
    planes = [at_feat(half, k, 0) for half in range(2) for k in range(1, 4)]
    barrier = pltpu.get_barrier_semaphore()
    for device in peers + planes:
        pl.semaphore_signal(barrier, inc=1, device_id=device, device_id_type=MESH)

    def sums(step, carry):
        out = []
        for v in range(2):
            values = views[v][pl.ds(pl.multiple_of(step * 64, 64), 64), :].astype(F32)
            out.append(carry[2 * v] + jnp.sum(values.reshape(8, 8, -1), axis=0))
            out.append(carry[2 * v + 1] + jnp.sum((values * values).reshape(8, 8, -1), axis=0))
        return tuple(out)

    zero = jnp.zeros((8, rows), F32)
    for load in loads:
        load.wait()
    parts = lax.fori_loop(0, rows // 64, sums, (zero,) * 4)
    for k in range(4):
        stat[batch, pl.ds(k, 1), :] = jnp.sum(parts[k], axis=0, keepdims=True)
    stat[batch, pl.ds(4, 4), :] = jnp.zeros((4, rows), F32)

    pl.semaphore_wait(barrier, len(peers) + len(planes))

    def exchange(ref, count=8):
        used = pl.ds(0, count)
        sender, receiver = net.sender(ref.at[pl.ds(0, 7), used]), net.receiver()
        for device in peers:
            send(ref.at[batch, used], ref.at[batch, used], sender, receiver, device)
        return receiver

    def collect(ref, receiver, count=8):
        wait(receiver, ref.at[pl.ds(0, 7), pl.ds(0, count)])
        result = ref[0]
        for k in range(1, 8):
            result = result + ref[k]
        return result

    stat_items = exchange(stat, 4)
    sibling = (batch + 1 - 2 * core, feat)
    half = rows // 2
    upper, lower = pl.ds(0, half), pl.ds(half, half)
    view_sends = [net.sender(raw.at[v, pl.ds(0, 7)]) for v in range(2)]
    view_sems = [[net.receiver() for _ in range(7)] for _ in range(2)]

    def send_rows(v, src, slot, device, part=None):
        dst = raw.at[v, slot] if part is None else raw.at[v, slot, part]
        send(src, dst, view_sends[v], view_sems[v][slot - 1], device)

    def wait_rows(v, slot):
        wait(view_sems[v][slot - 1], raw.at[v, slot])

    def send_near(v):
        send_rows(v, views[v], 6, at_batch(1, 0))
        send_rows(v, views[v], 2, at_batch(3, 0))

    send_near(1)
    for v in (1, 0):
        send_rows(v, views[v], 1, sibling)
    send_near(0)

    sum_all = collect(stat, stat_items, 4)
    for v in range(2):
        mean = sum_all[2 * v : 2 * v + 1] / total
        square = sum_all[2 * v + 1 : 2 * v + 2] / total
        moments[pl.ds(2 * v, 1), :] = mean
        moments[pl.ds(2 * v + 1, 1), :] = lax.rsqrt(square - mean * mean + 1e-05)

    def normalize(v, slot):
        source = views[v] if slot == 0 else raw.at[v, slot]

        @pl.loop(0, rows // 64)
        def _(step):
            here = pl.ds(pl.multiple_of(step * 64, 64), 64)
            values = source[here, :].astype(F32)
            unit = (values - moments[pl.ds(2 * v, 1), :]) * moments[pl.ds(2 * v + 1, 1), :]
            normed[v, slot, here, :] = unit.astype(BF16)

    def own_rows(v):
        normalize(v, 0)
        wait_rows(v, 1)
        normalize(v, 1)

    def near_rows(v):
        wait_rows(v, 6)
        wait_rows(v, 2)
        send_rows(v, raw.at[v, 2], 3, sibling)
        send_rows(v, raw.at[v, 6], 7, sibling)

    def take_near(v):
        normalize(v, 2)
        normalize(v, 6)
        for slot in (3, 7):
            wait_rows(v, slot)
            normalize(v, slot)

    def pass_far(v):
        send_rows(v, raw.at[v, 6, upper], 4, at_batch(1, 0), upper)
        send_rows(v, raw.at[v, 2, lower], 4, at_batch(3, 0), lower)

    def far_rows(v):
        wait_rows(v, 4)
        send_rows(v, raw.at[v, 4], 5, sibling)

    def take_far(v):
        normalize(v, 4)
        wait_rows(v, 5)
        normalize(v, 5)

    net.cross_sends = [net.sender(cross.at[v]) for v in range(2)]
    net.back_sends = [net.sender(back.at[v]) for v in range(2)]
    begun = set()

    def cross_rows(part, turn):
        return pl.ds(pl.multiple_of(lax.rem(part + turn, 2) * 256, 256), 256)

    def tile(step):
        return pl.ds(pl.multiple_of(step * 128, 128), 128)

    def partner(step):
        return rem4(step + 2 + (step // 2) * (1 + 2 * lax.rem(step, 2)))

    turned = x // 2

    def mirrored(left, right):
        return lax.dot_general(
            left.reshape(-1, left.shape[-1]), right, (((0,), (0,)), ((), ())), preferred_element_type=F32
        )

    def add(v, here, value):
        acc[v, here, :] = acc[v, here, :] + value if v in begun else value

    class Block:
        def __init__(self, v, kind):
            self.v, self.kind = v, kind
            base = (v * 3 + kind) * 5
            self.part, self.r1, self.r2, self.r3, self.full = blocks[base : base + 5]
            self.cross, self.back = cross.at[v], back.at[v]
            self.columns = REDUCED[kind]
            mirrored = 1 if kind == 2 else 0
            self.reduce_send = net.sender(self.part.at[pl.ds(0, 30)])
            self.gather_send = net.sender(self.full.at[pl.ds(0, 30 + mirrored)])
            self.sems = [net.receiver() for _ in range(7)]

        def mine(self, half):
            return (y, z) if half == 0 else (z, y)

        def product(self):
            v = self.v
            @pl.loop(0, 2)
            def _(step):
                def block(first, right, tile_rows=256, part=0):
                    start = pl.multiple_of(step * 256 + part * 128, 128)
                    left = normed[v, 0, pl.ds(start, tile_rows), :]
                    value = lax.dot_general(
                        left, right, (((1,), (1,)), ((), ())), preferred_element_type=F32
                    )
                    width = right.shape[0]
                    chunks = pl.ds(step * 16 + part * 8, tile_rows // 16)
                    self.part[chunks, :, pl.ds(first, width)] = value.astype(BF16).reshape(
                        tile_rows // 16, 16, width
                    )

                if self.kind == 0:
                    block(0, normed[v, 0, cross_rows(step, 0), :])
                    for part in range(2):
                        block(256, normed[v, 0, tile(partner(step * 2 + part)), :], 128, part)
                    block(384, normed[v, 1, cross_rows(step, core), :])
                elif self.kind == 1:
                    block(0, normed[v, 2])
                    block(rows, normed[v, 7])
                else:
                    block(0, normed[v, 4 + turned])

            for half in range(2):
                m1, _ = self.mine(half)
                base = half * 16 + rem4(m1 + 2) * 4
                for k in range(2):
                    send(
                        self.part.at[pl.ds(base + 2 * (1 - k), 2)],
                        self.r1.at[half, k],
                        self.reduce_send,
                        self.sems[0],
                        at_feat(half, 1 + 2 * k, 0),
                    )

        def pass_on(self):
            wait(self.sems[0], self.r1)
            for half in range(2):
                m1, _ = self.mine(half)
                for k in range(2):
                    base = half * 16 + rem4(m1 + 1 + 2 * k) * 4
                    here = pl.ds(base + 2 * (1 - k), 2)
                    self.part[here] = (
                        self.part[here].astype(F32) + self.r1[half, k].astype(F32)
                    ).astype(BF16)
                    send(
                        self.part.at[pl.ds(base, 4)],
                        self.r2.at[half, k],
                        self.reduce_send,
                        self.sems[1],
                        at_feat(half, 1 + 2 * k, 0),
                    )

        def turn(self):
            wait(self.sems[1], self.r2)
            for half in range(2):
                m1, m2 = self.mine(half)
                base = half * 16 + m1 * 4
                here = pl.ds(base, 4)
                self.part[here] = (
                    self.part[here].astype(F32)
                    + self.r2[half, 0].astype(F32)
                    + self.r2[half, 1].astype(F32)
                ).astype(BF16)
                for k in range(1, 4):
                    send(
                        self.part.at[base + rem4(m2 + k)],
                        self.r3.at[half, k - 1],
                        self.reduce_send,
                        self.sems[2],
                        at_feat(half, 0, k),
                    )

        def own(self, half):
            m1, m2 = self.mine(half)
            return half * 16 + m1 * 4 + m2

        def mirror(self, own, first, start, device):
            send(
                self.full.at[own, :, pl.ds(first, 512)],
                self.full.at[own, :, pl.ds(start, 512)],
                self.gather_send,
                self.sems[3],
                device,
            )

        def reduced(self):
            wait(self.sems[2], self.r3)
            for half in range(2):
                own = self.own(half)
                value = self.part[own].astype(F32)
                for k in range(3):
                    value = value + self.r3[half, k].astype(F32)
                self.full[own, :, pl.ds(0, self.columns)] = value.astype(BF16)
                if self.kind == 2:
                    self.mirror(own, 0, 512, at_batch(2, turned))
            if self.kind != 2:
                self.spread()

        def spread(self):
            if self.kind == 2:
                wait(self.sems[3], self.full.at[pl.ds(0, 1)])
            for half in range(2):
                here = self.full.at[self.own(half)]
                for k in range(1, 4):
                    send(here, here, self.gather_send, self.sems[4], at_feat(half, 0, k))

        def send_back(self, half, ahead, first, count):
            m1, _ = self.mine(half)
            chunks = pl.ds(half * 16 + rem4(m1 + ahead) * 4 + first, count)
            for k, device in enumerate((at_batch(1, 0), at_batch(3, 1))):
                send(
                    self.full.at[chunks, :, pl.ds(512 * k, 512)],
                    self.back.at[k, chunks],
                    net.back_sends[self.v],
                    self.sems[3],
                    device,
                )

        def gather(self):
            wait(self.sems[4], self.full.at[pl.ds(0, 6)])
            for half in range(2):
                m1, _ = self.mine(half)
                here = self.full.at[pl.ds(half * 16 + m1 * 4, 4)]
                for k in range(2):
                    send(here, here, self.gather_send, self.sems[5], at_feat(half, 1 + 2 * k, 0))
                if self.kind == 1:
                    self.send_back(half, 0, 0, 4)

        def gather_on(self):
            wait(self.sems[5], self.full.at[pl.ds(0, 16)])
            for half in range(2):
                m1, _ = self.mine(half)
                for k in range(2):
                    base = half * 16 + rem4(m1 + 3 + 2 * k) * 4
                    here = self.full.at[pl.ds(base + 2 * k, 2)]
                    send(here, here, self.gather_send, self.sems[6], at_feat(half, 1 + 2 * k, 0))
                    if self.kind == 1:
                        self.send_back(half, 3 + 2 * k, 0, 4)

        def arrived(self):
            wait(self.sems[6], self.full.at[pl.ds(0, 8)])
            if self.kind == 1:
                for half in range(2):
                    self.send_back(half, 2, 0, 4)

        def swap(self):
            self.arrived()
            send(
                self.full.at[:, :, pl.ds(384, 256)],
                self.cross,
                net.cross_sends[self.v],
                self.sems[3],
                sibling,
            )

        def apply(self):
            if self.kind == 0:
                wait(self.sems[3], self.cross)
            else:
                self.arrived()
            other = 1 - self.v
            if self.kind == 0:
                self.apply_own(other)
            else:

                @pl.loop(0, 2)
                def _(step):
                    here = pl.ds(pl.multiple_of(step * 256, 256), 256)

                    def direct(first, right):
                        left = self.full[pl.ds(step * 16, 16), :, pl.ds(first, 512)]
                        return jnp.dot(
                            left.reshape(256, 512), right, preferred_element_type=F32
                        )

                    if self.kind == 1:
                        value = direct(0, normed[other, 2]) + direct(rows, normed[other, 7])
                    else:
                        value = direct(0, normed[other, 4 + turned])
                        columns = pl.ds(pl.multiple_of(512 + step * 256, 256), 256)
                        left = self.full[:, :, columns]
                        value += mirrored(left, normed[other, 5 - turned])
                    add(other, here, value)

            begun.add(other)

        def apply_own(self, other):
            @pl.loop(0, rows // 128)
            def _(step):
                here = pl.ds(pl.multiple_of(step * 128, 128), 128)

                def direct(first, right):
                    width = right.shape[0]
                    left = self.full[pl.ds(step * 8, 8), :, pl.ds(first, width)]
                    return jnp.dot(
                        left.reshape(128, width), right, preferred_element_type=F32
                    )

                value = direct(0, normed[other, 0, cross_rows(step // 2, 0), :])
                value += direct(256, normed[other, 0, tile(partner(step)), :])
                value += direct(384, normed[other, 1, cross_rows(step // 2, core), :])
                taker = 3 - step + (step // 2) * (2 * step - 5)
                left = self.full[pl.ds(taker * 8, 8), :, pl.ds(256, 128)]
                value += mirrored(left, normed[other, 0, tile(taker), :])
                theirs = lax.rem(step // 2 + 1 - core, 2)
                first = pl.multiple_of(lax.rem(step, 2) * 128, 128)
                left = self.cross[pl.ds(theirs * 16, 16), :, pl.ds(first, 128)]
                value += mirrored(left, normed[other, 1, cross_rows(theirs, 0), :])
                add(other, here, value)

        def apply_back(self):
            wait(self.sems[3], self.back)
            other = 1 - self.v

            @pl.loop(0, 2)
            def _(step):
                here = pl.ds(pl.multiple_of(step * 256, 256), 256)
                value = mirrored(self.back[0, :, :, here], normed[other, 6])
                value += mirrored(self.back[1, :, :, here], normed[other, 3])
                add(other, here, value)

            begun.add(other)

        def stages(self):
            reduce = [self.product, self.pass_on, self.turn, self.reduced]
            if self.kind == 0:
                return reduce + [self.gather, self.gather_on, self.swap, self.apply]
            if self.kind == 1:
                return reduce + [self.gather, self.gather_on, self.apply, self.apply_back]
            return reduce + [self.spread, self.gather, self.gather_on, self.apply]

    same_items = []
    extras = []

    def diagonal():
        def step_sum(step, carry):
            here = pl.ds(pl.multiple_of(step * 64, 64), 64)
            both = normed[0, 0, here, :].astype(F32) * normed[1, 0, here, :].astype(F32)
            return carry + jnp.sum(both.reshape(8, 8, -1), axis=0)

        part = lax.fori_loop(0, rows // 64, step_sum, zero)
        same[batch] = part
        same_items.append(exchange(same))

    def unit_of(v, here):
        values = views[v][here, :].astype(F32)
        return (values - moments[pl.ds(2 * v, 1), :]) * moments[pl.ds(2 * v + 1, 1), :]

    def back_sums(v, last):
        def step_sum(step, carry):
            here = pl.ds(pl.multiple_of(step * 64, 64), 64)
            back = (2.0 * LAMBDA / total) * acc[v, here, :]
            back += extras[0] * normed[1 - v, 0, here, :].astype(F32)
            acc[v, here, :] = back
            first = carry[0] + jnp.sum(back.reshape(8, 8, -1), axis=0)
            second = carry[1] + jnp.sum((back * unit_of(v, here)).reshape(8, 8, -1), axis=0)
            return first, second

        first, second = lax.fori_loop(0, rows // 64, step_sum, (zero, zero))
        last[batch, pl.ds(0, 1), :] = jnp.sum(first, axis=0, keepdims=True)
        last[batch, pl.ds(1, 1), :] = jnp.sum(second, axis=0, keepdims=True)
        last[batch, pl.ds(2, 6), :] = jnp.zeros((6, rows), F32)
        return exchange(last, 2)

    def finish(v, last, items, out):
        both = collect(last, items, 2) / total
        first, second = both[0:1], both[1:2]

        @pl.loop(0, rows // 64)
        def _(step):
            here = pl.ds(pl.multiple_of(step * 64, 64), 64)
            out[here, :] = acc[v, here, :] - first - unit_of(v, here) * second

    plan = []

    def add_rows(name, ticks):
        plan.extend(zip(ticks, name))

    add_rows([lambda v=v: own_rows(v) for v in (1, 0)], ROWS[0])
    add_rows([diagonal], ROWS[1])
    for n, v in enumerate((1, 0)):
        steps = [lambda v=v, f=f: f(v) for f in (near_rows, take_near, pass_far, far_rows, take_far)]
        add_rows(steps, ROWS[2 + n])
    for v, kind, ticks in BLOCKS:
        add_rows(Block(v, kind).stages(), ticks)
    def early():
        cosine = jnp.sum(collect(same, same_items[0]), axis=0, keepdims=True) / total
        extra = (2.0 * (cosine - 1.0)).astype(BF16).astype(F32) - 2.0 * LAMBDA * cosine
        extras.append(extra)
        extras.append(back_sums(0, last_a))

    add_rows([early], (max(ticks[-1] for v, _, ticks in BLOCKS if v == 1),))
    for _, step in sorted(plan, key=lambda item: item[0]):
        step()
    items_b = back_sums(1, last_b)
    finish(0, last_a, extras[1], ga)
    finish(1, last_b, items_b, gb)
    net.finish()
    assert (len(net.sends), net.receives) == (SENDS, RECEIVES)


def body(view_a, view_b):
    rows, width = view_a.shape
    total = rows * lax.axis_size("batch")
    blocks = []
    for _ in range(2):
        for columns, wide in zip(REDUCED, GATHERED):
            blocks += [
                pltpu.VMEM((32, 16, columns), BF16),
                pltpu.VMEM((2, 2, 2, 16, columns), BF16),
                pltpu.VMEM((2, 2, 4, 16, columns), BF16),
                pltpu.VMEM((2, 3, 16, columns), BF16),
                pltpu.VMEM((32, 16, wide), BF16),
            ]
    vmem = pl.BlockSpec(memory_space=pltpu.VMEM)
    left_a, left_b, moments = pl.pallas_call(
        functools.partial(kernel, rows, total),
        out_shape=(pltpu.VMEM((rows, width), F32),) * 2 + (pltpu.VMEM((8, width), F32),),
        in_specs=[pl.BlockSpec(memory_space=pl.ANY)] * 2,
        out_specs=(vmem, vmem, vmem),
        scratch_shapes=[
            pltpu.VMEM((2, 8, rows, width), BF16),
            pltpu.VMEM((2, 8, rows, width), BF16),
            pltpu.VMEM((8, 8, width), F32),
            pltpu.VMEM((8, 8, width), F32),
            pltpu.VMEM((8, 8, width), F32),
            pltpu.VMEM((8, 8, width), F32),
            pltpu.VMEM((2, rows, width), F32),
            pltpu.VMEM((2, 32, 16, 256), BF16),
            pltpu.VMEM((2, 2, 32, 16, 512), BF16),
            pltpu.VMEM((2, rows, width), BF16),
            pltpu.SemaphoreType.DMA((2,)),
            pltpu.SemaphoreType.DMA((SENDS,)),
            pltpu.SemaphoreType.DMA((RECEIVES,)),
        ]
        + blocks,
        compiler_params=pltpu.CompilerParams(
            collective_id=0, has_side_effects=True, vmem_limit_bytes=56 * 2**20
        ),
        name="gram_gradient",
    )(view_a, view_b)
    return (moments[1] * left_a).astype(BF16), (moments[3] * left_b).astype(BF16)


def solution(mesh):
    return jax.shard_map(
        body,
        mesh=mesh,
        in_specs=(P("batch", "feat"), P("batch", "feat")),
        out_specs=(P("batch", "feat"), P("batch", "feat")),
        check_vma=False,
    )
```
